128 devices in a mesh: row: 16 (over y, z), col: 8 (over x, core).
Axes of the slice: x: 4, y: 4, z: 4, core: 2. Of those that a mesh axis runs over, the one named last changes fastest.
Arguments:
- amplitudes: float32 [128, 512, 512], P(('row', 'col')), may hold values from -6 to 6
- integrals: float32 [512, 1024, 1024], P(('row', 'col')), may hold values from -0.01171875 to 0.01171875
- coupling: float32 [512, 32, 1024], P(('row', 'col')), may hold values from -0.046875 to 0.046875
- task_table: int32 [128, 4, 2], replicated, may hold values from -1 to 15, as said below
Outputs:
- residual: float32 [128, 1024], P(('row', 'col'))
The draws below stay inside these ranges and needn't reach their ends.
Inputs may be any that keep to these rules, and one draw needn't show every extreme that they name: `task_table`: every virtual tile pair (C, D), C and D in 0 to 15, appears in exactly one slot. In each device's row the valid slots come first and the rest hold -1 in both entries. Some device has all 4 slots valid and some device has none. `integrals`: slots that task_table marks -1 are not read.
All inputs are finite; a program needn't handle non-finite values.
Results may differ from the reference program's by a relative error of at most 0.0003.
Values sent between devices are 32-bit elements; how exact they have to be, the bound alone decides.
No kernel may reach another device: no remote copies, remote signals or barrier semaphores. Data moves between devices by JAX's collectives and lax.ppermute only.
A program may use at most 128 MiB of HBM per device.

```python
import jax
import jax.numpy as jnp
from jax import lax

O = 32
V = 512
TB = 32
OW = 4
NVT = 16
TILES = 256
SLOTS = 4
SLOTS_ALL = 512
ROWS = 128
DEVICES = 128


def draw_task_table(key, part):
    first, second, third = jax.random.split(jax.random.fold_in(key, 11), 3)
    halves = DEVICES // 2
    split_sizes = jax.random.randint(first, (halves,), 0, SLOTS + 1).astype(jnp.int32)
    split_sizes = split_sizes.at[0].set(SLOTS)
    paired = jnp.stack([split_sizes, SLOTS - split_sizes], axis=1).reshape(DEVICES)
    device_order = jax.random.permutation(second, DEVICES)
    tallies = jnp.zeros((DEVICES,), jnp.int32).at[device_order].set(paired)
    offsets = jnp.cumsum(tallies) - tallies
    shuffled = jax.random.permutation(third, TILES).astype(jnp.int32)
    slot_range = jnp.arange(SLOTS, dtype=jnp.int32)
    positions = jnp.clip(offsets[:, None] + slot_range[None, :], 0, TILES - 1)
    valid = slot_range[None, :] < tallies[:, None]
    chosen = shuffled[positions]
    upper = jnp.where(valid, chosen // NVT, -1)
    lower = jnp.where(valid, chosen % NVT, -1)
    return jnp.stack([upper, lower], axis=-1).astype(jnp.int32)


def levels(rng, extent, cuts, smallest, largest):
    factor_of, own = 1.0, jax.random.fold_in(rng, 6)
    for position, shards_of in cuts:
        draws = jnp.exp(jax.random.uniform(jax.random.fold_in(own, position), (shards_of,), jnp.float32, smallest / len(cuts), largest / len(cuts)))
        factor_of = factor_of * jnp.repeat(draws, extent[position] // shards_of).reshape([-1 if axis == position else 1 for axis in range(len(extent))])
    return factor_of


def centred(own_key, shape, scale, reach, cuts=(), kind=jnp.bfloat16):
    factor_of = levels(own_key, shape, cuts, -0.22, 0.18) if cuts else 1.0
    values = jax.random.normal(own_key, shape, jnp.float32) * scale * factor_of
    return jnp.minimum(jnp.maximum(values, -reach), reach).astype(kind)


def setup_inputs(seed: int = 0) -> dict:
    arg_keys = jax.random.split(jax.random.key(seed), 5)
    amplitudes = centred(arg_keys[0], (ROWS, V, V), 1.0, 6.0, ((0, 128),), jnp.float32)
    integrals = centred(arg_keys[1], (SLOTS_ALL, TB * TB, TB * TB), (V * V) ** -0.5, 0.01171875, ((0, 128),), jnp.float32)
    coupling = centred(arg_keys[2], (V, O, O * TB), (V * O) ** -0.5, 0.046875, ((0, 128),), jnp.float32)
    task_table = draw_task_table(jax.random.fold_in(arg_keys[4], 71), 0)
    return dict(amplitudes=amplitudes, integrals=integrals, coupling=coupling, task_table=task_table)


def reference(amplitudes, integrals, coupling, task_table):
    flat = task_table.reshape(SLOTS_ALL, 2)
    valid = flat[:, 0] >= 0
    pair_ids = jnp.where(valid, flat[:, 0] * NVT + flat[:, 1], TILES).astype(jnp.int32)
    inverse = jnp.zeros((TILES + 1,), jnp.int32).at[pair_ids].set(jnp.arange(SLOTS_ALL, dtype=jnp.int32))[:TILES]

    def add_pair(partial_value, tile_index):
        upper = ((tile_index // NVT) * TB).astype(jnp.int32)
        lower = ((tile_index % NVT) * TB).astype(jnp.int32)
        columns = lax.dynamic_slice(amplitudes, (jnp.int32(0), upper, lower), (ROWS, TB, TB)).reshape(ROWS, TB * TB)
        integral_tile = integrals[inverse[tile_index]]
        product = lax.dot_general(columns, integral_tile, (((1,), (1,)), ((), ())), precision=lax.Precision.HIGHEST, preferred_element_type=jnp.float32)
        return partial_value + product, None

    ladder, _ = lax.scan(add_pair, jnp.zeros((ROWS, TB * TB), jnp.float32), jnp.arange(TILES, dtype=jnp.int32))
    regrouped = jnp.transpose(amplitudes[:, :TB, :].reshape(OW, O, TB, V), (0, 2, 3, 1)).reshape(OW * TB, V * O)
    hole_term = jnp.dot(regrouped, coupling.reshape(V * O, O * TB), precision=lax.Precision.HIGHEST, preferred_element_type=jnp.float32)
    hole_term = jnp.transpose(hole_term.reshape(OW, TB, O, TB), (0, 2, 1, 3)).reshape(ROWS, TB * TB)
    return ladder + hole_term
```

```python
import functools

import jax
import jax.numpy as jnp
from jax import lax
from jax.experimental import pallas as pl
from jax.experimental.pallas import tpu as pltpu
from jax.sharding import Mesh
from jax.sharding import PartitionSpec as P

TB = 32
NVT = 16
SLOTS = 4
DEVICES = 128
V = 512
PAIR = TB * TB
LANES = 128
MSG = SLOTS * 8 + 1
ROW_COL = ("row_0", "row_1", "col_0", "col_1")
F32 = jnp.float32
BF16 = jnp.bfloat16


def exchange_chunks(parts):
    lane = lax.broadcasted_iota(jnp.int32, parts[0].shape, parts[0].ndim - 1)
    odd = (lane // TB) % 2 == 1
    high = lane >= 2 * TB
    axis = parts[0].ndim - 1

    def swap(a, b, mask, shift):
        return (
            jnp.where(mask, pltpu.roll(b, shift, axis), a),
            jnp.where(mask, b, pltpu.roll(a, LANES - shift, axis)),
        )

    c0, c1 = swap(parts[0], parts[1], odd, TB)
    c2, c3 = swap(parts[2], parts[3], odd, TB)
    b0, b2 = swap(c0, c2, high, 2 * TB)
    b1, b3 = swap(c1, c3, high, 2 * TB)
    return b0, b1, b2, b3


def pack_kernel(table_ref, amp0_ref, amp1_ref, amp2_ref, amp3_ref, send_ref, stacked_ref, turned_ref):
    amp_refs = (amp0_ref, amp1_ref, amp2_ref, amp3_ref)

    def relayout(upper, _):
        row = pl.multiple_of(upper * TB, TB)
        for group in range(V // LANES):
            parts = [amp_refs[group][pl.ds(row + k, 8, stride=4), :] for k in range(4)]
            for h, tile in enumerate(exchange_chunks(parts)):
                stacked_ref[upper * NVT + group * 4 + h] = tile
        return 0

    lax.fori_loop(0, NVT, relayout, 0)

    def place(q, _):
        for s in range(SLOTS):
            pair = jnp.maximum(table_ref[s, 0, q] * NVT + table_ref[s, 1, q], 0)
            send_ref[pl.ds(q * MSG + s * 8, 8), :] = stacked_ref[pair]
        return 0

    lax.fori_loop(0, DEVICES, place, 0, unroll=4)
    for group in range(V // LANES):
        turned_ref[pl.ds(group * LANES, LANES), 0:TB] = amp_refs[group][0:TB, :].T
    parts = [turned_ref[pl.ds(k, DEVICES, stride=4), :] for k in range(4)]
    send_ref[pl.ds(SLOTS * 8, DEVICES, stride=MSG), :] = exchange_chunks(parts)[0]


def pack(table, amplitudes):
    return pl.pallas_call(
        pack_kernel,
        out_shape=jax.ShapeDtypeStruct((DEVICES * MSG, LANES), F32),
        in_specs=[
            pl.BlockSpec(memory_space=pltpu.SMEM),
            *[pl.BlockSpec((V, LANES), functools.partial(lambda g, _: (0, g), g)) for g in range(4)],
        ],
        grid=(1,),
        out_specs=pl.BlockSpec((DEVICES * MSG, LANES), lambda _: (0, 0)),
        scratch_shapes=[
            pltpu.VMEM((NVT * NVT, 8, LANES), F32),
            pltpu.VMEM((V, LANES), F32),
        ],
        compiler_params=pltpu.CompilerParams(vmem_limit_bytes=16 * 1024 * 1024),
        name="pack",
    )(table, *[amplitudes] * 4)


def split_parts(value):
    high = value.astype(BF16)
    return high, (value - high.astype(F32)).astype(BF16)


CHUNK = 256
CHUNKS = PAIR // CHUNK


def split_kernel(count_ref, int_ref, high_ref, low_ref):
    slot = pl.program_id(0)

    @pl.when(slot < count_ref[0])
    def _():
        high, low = split_parts(int_ref[...])
        high_ref[...] = high
        low_ref[...] = low


def split_integrals(count, integrals):
    def place(slot, chunk, count_ref):
        used = slot < count_ref[0]
        last = jnp.maximum(count_ref[0] - 1, 0)
        return jnp.where(used, slot, last), jnp.where(used, chunk, CHUNKS - 1), 0

    spec = pl.BlockSpec((1, CHUNK, PAIR), place)
    shape = jax.ShapeDtypeStruct((SLOTS, PAIR, PAIR), BF16)
    return pl.pallas_call(
        split_kernel,
        out_shape=(shape, shape),
        grid_spec=pltpu.PrefetchScalarGridSpec(
            num_scalar_prefetch=1, grid=(SLOTS, CHUNKS), in_specs=[spec], out_specs=[spec, spec]
        ),
        compiler_params=pltpu.CompilerParams(vmem_limit_bytes=16 * 1024 * 1024),
        cost_estimate=pl.CostEstimate(
            flops=SLOTS * PAIR * PAIR, bytes_accessed=SLOTS * PAIR * PAIR * 8, transcendentals=0
        ),
        name="split",
    )(count, integrals)


def nt_dot(a, b):
    return lax.dot_general(a, b, (((1,), (1,)), ((), ())), preferred_element_type=F32)


def tn_dot(a, b):
    return lax.dot_general(a, b, (((0,), (0,)), ((), ())), preferred_element_type=F32)


def main_kernel(count_ref, recv_ref, high_ref, low_ref, coup_ref, out_ref, both_ref, acc_ref, hole_ref):
    slot = pl.program_id(0)
    count = count_ref[0]

    @pl.when(slot == 0)
    def _():
        acc_ref[...] = jnp.zeros_like(acc_ref)

    @pl.when(slot < count)
    def _():
        for m in range(8):
            part = recv_ref[pl.ds(slot * 8 + m, DEVICES, stride=MSG), :]
            high, low = split_parts(part)
            both_ref[0:DEVICES, m * LANES : (m + 1) * LANES] = high
            both_ref[DEVICES:, m * LANES : (m + 1) * LANES] = low
        for chunk in range(CHUNKS):
            rows = slice(chunk * CHUNK, (chunk + 1) * CHUNK)
            top = nt_dot(both_ref[...], high_ref[0, rows, :])
            low = nt_dot(both_ref[0:DEVICES, :], low_ref[0, rows, :])
            acc_ref[:, rows] += top[:DEVICES] + top[DEVICES:] + low

    @pl.when(slot == SLOTS - 1)
    def _():
        data = recv_ref[pl.ds(SLOTS * 8, DEVICES, stride=MSG), :]
        blocks = exchange_chunks([data[i * TB : (i + 1) * TB] for i in range(4)])
        left_high, left_low = split_parts(jnp.concatenate(blocks, axis=0))
        right_high, right_low = split_parts(coup_ref[...])
        hole = tn_dot(left_high, right_high) + tn_dot(left_low, right_high) + tn_dot(left_high, right_low)
        for group in range(8):
            hole_ref[group] = hole[:, group * LANES : (group + 1) * LANES]
        for m in range(8):
            out_ref[pl.ds(m, DEVICES, stride=8), :] = acc_ref[:, m * LANES : (m + 1) * LANES]
        for i in range(4):
            for group in range(8):
                parts = [hole_ref[group, pl.ds(i * TB + k, 8, stride=4), :] for k in range(4)]
                for h, tile in enumerate(exchange_chunks(parts)):
                    row = (i * TB + group * 4 + h) * 8
                    out_ref[row : row + 8, :] += tile


def partial_residual(count, received, high, low, coupling):
    def place(slot, count_ref):
        return jnp.minimum(slot, jnp.maximum(count_ref[0] - 1, 0)), 0, 0

    spec = pl.BlockSpec((1, PAIR, PAIR), place)
    whole = lambda slot, count_ref: (0, 0)
    return pl.pallas_call(
        main_kernel,
        out_shape=jax.ShapeDtypeStruct((DEVICES * 8, LANES), F32),
        grid_spec=pltpu.PrefetchScalarGridSpec(
            num_scalar_prefetch=1,
            grid=(SLOTS,),
            in_specs=[
                pl.BlockSpec((DEVICES * MSG, LANES), whole),
                spec,
                spec,
                pl.BlockSpec((LANES, PAIR), whole),
            ],
            out_specs=pl.BlockSpec((DEVICES * 8, LANES), whole),
            scratch_shapes=[
                pltpu.VMEM((2 * DEVICES, PAIR), BF16),
                pltpu.VMEM((DEVICES, PAIR), F32),
                pltpu.VMEM((8, DEVICES, LANES), F32),
            ],
        ),
        compiler_params=pltpu.CompilerParams(vmem_limit_bytes=32 * 1024 * 1024),
        name="residual",
    )(count, received, high, low, coupling)


def body(amplitudes, integrals, coupling, task_table):
    table = jnp.transpose(task_table, (1, 2, 0))
    counts = jnp.sum((table[:, 0, :] >= 0).astype(jnp.int32), axis=0)
    count = lax.dynamic_slice(counts, (lax.axis_index(ROW_COL),), (1,))
    outgoing = pack(table, amplitudes.reshape(V, V))
    received = lax.all_to_all(
        outgoing.reshape(DEVICES, MSG, 1, LANES), ROW_COL, split_axis=0, concat_axis=0, tiled=True
    ).reshape(DEVICES * MSG, LANES)
    high, low = split_integrals(count, integrals)
    partial = partial_residual(count, received, high, low, coupling.reshape(LANES, PAIR))
    terms = lax.all_to_all(partial.reshape(DEVICES, 8, LANES), ROW_COL, split_axis=0, concat_axis=0, tiled=True)
    return jnp.sum(terms, axis=0).reshape(1, PAIR)


def solution(mesh):
    split = Mesh(mesh.devices.reshape(4, 4, 4, 2), ("row_0", "row_1", "col_0", "col_1"))
    in_specs = (P(ROW_COL, None, None), P(ROW_COL, None, None), P(ROW_COL, None, None), P())
    return jax.shard_map(body, mesh=split, in_specs=in_specs, out_specs=P(ROW_COL, None), check_vma=False)
```

```python
import functools

import jax
import jax.numpy as jnp
from jax import lax
from jax.experimental import pallas as pl
from jax.experimental.pallas import tpu as pltpu
from jax.sharding import Mesh
from jax.sharding import PartitionSpec as P

TB = 32
NVT = 16
SLOTS = 4
DEVICES = 128
V = 512
PAIR = TB * TB
LANES = 128
MSG = SLOTS * 8 + 1
ROW_COL = ("row_0", "row_1", "col_0", "col_1")
F32 = jnp.float32
BF16 = jnp.bfloat16


def exchange_chunks(parts):
    lane = lax.broadcasted_iota(jnp.int32, parts[0].shape, parts[0].ndim - 1)
    odd = (lane // TB) % 2 == 1
    high = lane >= 2 * TB
    axis = parts[0].ndim - 1

    def swap(a, b, mask, shift):
        return (
            jnp.where(mask, pltpu.roll(b, shift, axis), a),
            jnp.where(mask, b, pltpu.roll(a, LANES - shift, axis)),
        )

    c0, c1 = swap(parts[0], parts[1], odd, TB)
    c2, c3 = swap(parts[2], parts[3], odd, TB)
    b0, b2 = swap(c0, c2, high, 2 * TB)
    b1, b3 = swap(c1, c3, high, 2 * TB)
    return b0, b1, b2, b3


QUARTERS = V // LANES
TILES = NVT * NVT


def pack_kernel(table_hbm, amp_hbm, send_ref, table_ref, row_ref, place_ref, amp_ref, turned_ref, sems):
    table_copy = pltpu.make_async_copy(table_hbm, table_ref, sems.at[QUARTERS])
    table_copy.start()
    copies = []
    for group in range(QUARTERS):
        lanes = pl.ds(group * LANES, LANES)
        copies.append(pltpu.make_async_copy(amp_hbm.at[:, lanes], amp_ref.at[group], sems.at[group]))
        copies[-1].start()
    table_copy.wait()
    sublane = lax.broadcasted_iota(jnp.int32, (8, DEVICES), 0)
    device = lax.broadcasted_iota(jnp.int32, (8, DEVICES), 1)
    tiles = lax.broadcasted_iota(jnp.int32, (TILES, DEVICES), 0)
    found = jnp.zeros((8, TILES), F32)
    for s in range(SLOTS):
        pair = table_ref[s, 0:1, :] * NVT + table_ref[s, 1:2, :]
        match = (tiles == pair).astype(F32).astype(BF16)
        found += nt_dot(jnp.where(sublane == 0, device, s).astype(F32).astype(BF16), match)
    row_ref[...] = (found[0:1] * MSG + found[1:2] * 8).astype(jnp.int32)
    row_copy = pltpu.make_async_copy(row_ref, place_ref, sems.at[QUARTERS])
    row_copy.start()
    copies[0].wait()
    row_copy.wait()
    for group in range(QUARTERS):
        if group:
            copies[group].wait()
        parts = [amp_ref[group, pl.ds(k, DEVICES, stride=4), :] for k in range(4)]
        for h, tiles in enumerate(exchange_chunks(parts)):
            for upper in range(NVT):
                row = place_ref[0, upper * NVT + group * 4 + h]
                send_ref[pl.ds(row, 8), :] = tiles[upper * 8 : (upper + 1) * 8]
        turned_ref[pl.ds(group * LANES, LANES), 0:TB] = amp_ref[group, 0:TB, :].T
    parts = [turned_ref[pl.ds(k, DEVICES, stride=4), :] for k in range(4)]
    send_ref[pl.ds(SLOTS * 8, DEVICES, stride=MSG), :] = exchange_chunks(parts)[0]


def pack(table, amplitudes):
    hbm = pl.BlockSpec(memory_space=pltpu.HBM)
    return pl.pallas_call(
        pack_kernel,
        out_shape=jax.ShapeDtypeStruct((DEVICES * MSG, LANES), F32),
        in_specs=[hbm, hbm],
        out_specs=pl.BlockSpec(memory_space=pltpu.VMEM),
        scratch_shapes=[
            pltpu.VMEM((SLOTS, 2, DEVICES), jnp.int32),
            pltpu.VMEM((1, TILES), jnp.int32),
            pltpu.SMEM((1, TILES), jnp.int32),
            pltpu.VMEM((QUARTERS, V, LANES), F32),
            pltpu.VMEM((V, LANES), F32),
            pltpu.SemaphoreType.DMA((QUARTERS + 1,)),
        ],
        compiler_params=pltpu.CompilerParams(vmem_limit_bytes=16 * 1024 * 1024),
        name="pack",
    )(
        pltpu.with_memory_space_constraint(table, pltpu.HBM),
        pltpu.with_memory_space_constraint(amplitudes, pltpu.HBM),
    )


def nt_dot(a, b):
    return lax.dot_general(a, b, (((1,), (1,)), ((), ())), preferred_element_type=F32)


def nn_dot(a, b):
    return lax.dot_general(a, b, (((1,), (0,)), ((), ())), preferred_element_type=F32)


def split_parts(value):
    high = value.astype(BF16)
    return high, (value - high.astype(F32)).astype(BF16)


PIECE = 256


def main_kernel(table_hbm, recv_ref, int_hbm, coup_ref, out_ref, table_ref, int_ref, both_ref, acc_ref, hole_ref, sems):
    def fetch(slot):
        return pltpu.make_async_copy(int_hbm.at[slot], int_ref.at[slot], sems.at[slot])

    fetch(0).start()
    table_copy = pltpu.make_async_copy(table_hbm, table_ref, sems.at[SLOTS])
    table_copy.start()
    data = recv_ref[pl.ds(SLOTS * 8, DEVICES, stride=MSG), :]
    blocks = exchange_chunks([data[i * TB : (i + 1) * TB] for i in range(4)])
    left_high, left_low = split_parts(jnp.concatenate(blocks, axis=0).T)
    right_high, right_low = split_parts(coup_ref[...])
    hole = nn_dot(left_high, right_high) + nn_dot(left_low, right_high) + nn_dot(left_high, right_low)
    for group in range(8):
        hole_ref[group] = hole[:, group * LANES : (group + 1) * LANES]
    for group in range(8):
        parts = [hole_ref[group, pl.ds(k, DEVICES // 4, stride=4), :] for k in range(4)]
        for h, tiles in enumerate(exchange_chunks(parts)):
            for i in range(4):
                row = (i * TB + group * 4 + h) * 8
                out_ref[row : row + 8, :] = tiles[i * 8 : (i + 1) * 8]

    table_copy.wait()
    own = lax.axis_index(ROW_COL)
    count = jnp.int32(0)
    for s in range(SLOTS):
        count += (table_ref[s, 0, own] >= 0).astype(jnp.int32)

    @pl.when(count > 1)
    def _():
        fetch(1).start()

    acc_ref[...] = jnp.zeros_like(acc_ref)

    def prepare(slot, _):
        for m in range(8):
            high, low = split_parts(recv_ref[pl.ds(slot * 8 + m, DEVICES, stride=MSG), :])
            both_ref[slot, 0:DEVICES, m * LANES : (m + 1) * LANES] = high
            both_ref[slot, DEVICES:, m * LANES : (m + 1) * LANES] = low
        return 0

    lax.fori_loop(0, count, prepare, 0)
    fetch(0).wait()

    def add_slot(slot, _):
        @pl.when(slot > 0)
        def _():
            fetch(slot).wait()

        @pl.when(slot + 2 < count)
        def _():
            fetch(slot + 2).start()

        for piece in range(PAIR // PIECE):
            rows = slice(piece * PIECE, (piece + 1) * PIECE)
            int_high, int_low = split_parts(int_ref[slot, rows, :])
            top = nt_dot(int_high, both_ref[slot])
            low = nt_dot(int_low, both_ref[slot, 0:DEVICES, :])
            acc_ref[rows, :] += top[:, :DEVICES] + top[:, DEVICES:] + low
        return 0

    lax.fori_loop(0, count, add_slot, 0)
    for m in range(8):
        out_ref[pl.ds(m, DEVICES, stride=8), :] += acc_ref[m * LANES : (m + 1) * LANES, :].T


def partial_residual(table, received, integrals, coupling):
    whole = pl.BlockSpec(memory_space=pltpu.VMEM)
    hbm = pl.BlockSpec(memory_space=pltpu.HBM)
    return pl.pallas_call(
        main_kernel,
        out_shape=jax.ShapeDtypeStruct((DEVICES * 8, LANES), F32),
        in_specs=[hbm, whole, hbm, whole],
        out_specs=whole,
        scratch_shapes=[
            pltpu.SMEM((SLOTS, 2, DEVICES), jnp.int32),
            pltpu.VMEM((SLOTS, PAIR, PAIR), F32),
            pltpu.VMEM((SLOTS, 2 * DEVICES, PAIR), BF16),
            pltpu.VMEM((PAIR, DEVICES), F32),
            pltpu.VMEM((8, DEVICES, LANES), F32),
            pltpu.SemaphoreType.DMA((SLOTS + 1,)),
        ],
        compiler_params=pltpu.CompilerParams(vmem_limit_bytes=40 * 1024 * 1024),
        name="residual",
    )(pltpu.with_memory_space_constraint(table, pltpu.HBM), received, pltpu.with_memory_space_constraint(integrals, pltpu.HBM), coupling)


def body(amplitudes, integrals, coupling, task_table):
    table = jnp.transpose(task_table, (1, 2, 0))
    outgoing = pack(table, amplitudes.reshape(V, V))
    received = lax.all_to_all(
        outgoing.reshape(DEVICES, MSG, 1, LANES), ROW_COL, split_axis=0, concat_axis=0, tiled=True
    ).reshape(DEVICES * MSG, LANES)
    partial = partial_residual(table, received, integrals, coupling.reshape(LANES, PAIR))
    terms = lax.all_to_all(partial.reshape(DEVICES, 8, LANES), ROW_COL, split_axis=0, concat_axis=0, tiled=True)
    return jnp.sum(terms, axis=0).reshape(1, PAIR)


def solution(mesh):
    split = Mesh(mesh.devices.reshape(4, 4, 4, 2), ("row_0", "row_1", "col_0", "col_1"))
    in_specs = (P(ROW_COL, None, None), P(ROW_COL, None, None), P(ROW_COL, None, None), P())
    return jax.shard_map(body, mesh=split, in_specs=in_specs, out_specs=P(ROW_COL, None), check_vma=False)
```

```python
import functools

import jax
import jax.numpy as jnp
from jax import lax
from jax.experimental import pallas as pl
from jax.experimental.pallas import tpu as pltpu
from jax.sharding import Mesh
from jax.sharding import PartitionSpec as P

TB = 32
NVT = 16
SLOTS = 4
DEVICES = 128
V = 512
PAIR = TB * TB
LANES = 128
MSG = SLOTS * 8 + 1
ROW_COL = ("row_0", "row_1", "col_0", "col_1")
F32 = jnp.float32
BF16 = jnp.bfloat16


def exchange_chunks(parts):
    lane = lax.broadcasted_iota(jnp.int32, parts[0].shape, parts[0].ndim - 1)
    odd = (lane // TB) % 2 == 1
    high = lane >= 2 * TB
    axis = parts[0].ndim - 1

    def swap(a, b, mask, shift):
        return (
            jnp.where(mask, pltpu.roll(b, shift, axis), a),
            jnp.where(mask, b, pltpu.roll(a, LANES - shift, axis)),
        )

    c0, c1 = swap(parts[0], parts[1], odd, TB)
    c2, c3 = swap(parts[2], parts[3], odd, TB)
    b0, b2 = swap(c0, c2, high, 2 * TB)
    b1, b3 = swap(c1, c3, high, 2 * TB)
    return b0, b1, b2, b3


QUARTERS = V // LANES
TILES = NVT * NVT


def pack_kernel(
    table_hbm, amp_hbm, int_hbm, send_ref, head_ref, table_ref, row_ref, place_ref, amp_ref, turned_ref, sems
):
    head_copy = pltpu.make_async_copy(int_hbm.at[0], head_ref, sems.at[QUARTERS + 1])
    table_copy = pltpu.make_async_copy(table_hbm, table_ref, sems.at[QUARTERS])
    table_copy.start()
    copies = []
    for group in range(QUARTERS):
        lanes = pl.ds(group * LANES, LANES)
        copies.append(pltpu.make_async_copy(amp_hbm.at[:, lanes], amp_ref.at[group], sems.at[group]))
        copies[-1].start()
    head_copy.start()
    table_copy.wait()
    sublane = lax.broadcasted_iota(jnp.int32, (8, DEVICES), 0)
    device = lax.broadcasted_iota(jnp.int32, (8, DEVICES), 1)
    tiles = lax.broadcasted_iota(jnp.int32, (TILES, DEVICES), 0)
    found = jnp.zeros((8, TILES), F32)
    for s in range(SLOTS):
        pair = table_ref[s, 0:1, :] * NVT + table_ref[s, 1:2, :]
        match = (tiles == pair).astype(F32).astype(BF16)
        found += nt_dot(jnp.where(sublane == 0, device, s).astype(F32).astype(BF16), match)
    row_ref[...] = (found[0:1] * MSG + found[1:2] * 8).astype(jnp.int32)
    row_copy = pltpu.make_async_copy(row_ref, place_ref, sems.at[QUARTERS])
    row_copy.start()
    copies[0].wait()
    row_copy.wait()
    for group in range(QUARTERS):
        if group:
            copies[group].wait()
        parts = [amp_ref[group, pl.ds(k, DEVICES, stride=4), :] for k in range(4)]
        for h, tiles in enumerate(exchange_chunks(parts)):
            for upper in range(NVT):
                row = place_ref[0, upper * NVT + group * 4 + h]
                send_ref[pl.ds(row, 8), :] = tiles[upper * 8 : (upper + 1) * 8]
        turned_ref[pl.ds(group * LANES, LANES), 0:TB] = amp_ref[group, 0:TB, :].T
    parts = [turned_ref[pl.ds(k, DEVICES, stride=4), :] for k in range(4)]
    send_ref[pl.ds(SLOTS * 8, DEVICES, stride=MSG), :] = exchange_chunks(parts)[0]
    head_copy.wait()


def pack(table, amplitudes, integrals):
    hbm = pl.BlockSpec(memory_space=pltpu.HBM)
    return pl.pallas_call(
        pack_kernel,
        out_shape=(
            jax.ShapeDtypeStruct((DEVICES * MSG, LANES), F32),
            jax.ShapeDtypeStruct((PAIR, PAIR), F32),
        ),
        in_specs=[hbm, hbm, hbm],
        out_specs=(pl.BlockSpec(memory_space=pltpu.VMEM),) * 2,
        scratch_shapes=[
            pltpu.VMEM((SLOTS, 2, DEVICES), jnp.int32),
            pltpu.VMEM((1, TILES), jnp.int32),
            pltpu.SMEM((1, TILES), jnp.int32),
            pltpu.VMEM((QUARTERS, V, LANES), F32),
            pltpu.VMEM((V, LANES), F32),
            pltpu.SemaphoreType.DMA((QUARTERS + 2,)),
        ],
        compiler_params=pltpu.CompilerParams(vmem_limit_bytes=16 * 1024 * 1024),
        name="pack",
    )(
        pltpu.with_memory_space_constraint(table, pltpu.HBM),
        pltpu.with_memory_space_constraint(amplitudes, pltpu.HBM),
        pltpu.with_memory_space_constraint(integrals, pltpu.HBM),
    )


def nt_dot(a, b):
    return lax.dot_general(a, b, (((1,), (1,)), ((), ())), preferred_element_type=F32)


def nn_dot(a, b):
    return lax.dot_general(a, b, (((1,), (0,)), ((), ())), preferred_element_type=F32)


def split_parts(value):
    high = value.astype(BF16)
    return high, (value - high.astype(F32)).astype(BF16)


PIECE = 256


def main_kernel(
    table_hbm,
    recv_ref,
    head_ref,
    int_hbm,
    coup_ref,
    out_ref,
    table_ref,
    int_ref,
    both_ref,
    acc_ref,
    hole_ref,
    sems,
):
    table_copy = pltpu.make_async_copy(table_hbm, table_ref, sems.at[SLOTS])
    table_copy.start()

    def fetch(slot):
        return pltpu.make_async_copy(int_hbm.at[slot], int_ref.at[slot - 1], sems.at[slot])

    fetch(1).start()

    def prepare(slot):
        for m in range(8):
            high, low = split_parts(recv_ref[pl.ds(slot * 8 + m, DEVICES, stride=MSG), :])
            both_ref[slot, 0:DEVICES, m * LANES : (m + 1) * LANES] = high
            both_ref[slot, DEVICES:, m * LANES : (m + 1) * LANES] = low

    def product(slot, values):
        int_high, int_low = split_parts(values)
        top = nt_dot(int_high, both_ref[slot])
        low = nt_dot(int_low, both_ref[slot, 0:DEVICES, :])
        return top[:, :DEVICES] + top[:, DEVICES:] + low

    pieces = [slice(first, first + PIECE) for first in range(0, PAIR, PIECE)]
    prepare(0)
    table_copy.wait()
    own = lax.axis_index(ROW_COL)
    count = jnp.int32(0)
    for s in range(SLOTS):
        count += (table_ref[s, 0, own] >= 0).astype(jnp.int32)
    for slot in range(2, SLOTS):

        @pl.when(slot < count)
        def _():
            fetch(slot).start()

    data = recv_ref[pl.ds(SLOTS * 8, DEVICES, stride=MSG), :]
    blocks = exchange_chunks([data[i * TB : (i + 1) * TB] for i in range(4)])
    left_high, left_low = split_parts(jnp.concatenate(blocks, axis=0).T)
    right_high, right_low = split_parts(coup_ref[...])
    hole = nn_dot(left_high, right_high) + nn_dot(left_low, right_high) + nn_dot(left_high, right_low)
    for group in range(8):
        hole_ref[group] = hole[:, group * LANES : (group + 1) * LANES]
    for group in range(8):
        parts = [hole_ref[group, pl.ds(k, DEVICES // 4, stride=4), :] for k in range(4)]
        for h, tiles in enumerate(exchange_chunks(parts)):
            for i in range(4):
                row = (i * TB + group * 4 + h) * 8
                out_ref[row : row + 8, :] = tiles[i * 8 : (i + 1) * 8]

    for rows in pieces:
        acc_ref[rows, :] = jnp.where(count > 0, product(0, head_ref[rows, :]), 0.0)
    fetch(1).wait()

    def add_slot(slot, _):
        prepare(slot)

        @pl.when(slot > 1)
        def _():
            fetch(slot).wait()

        for rows in pieces:
            acc_ref[rows, :] += product(slot, int_ref[slot - 1, rows, :])
        return 0

    lax.fori_loop(1, count, add_slot, 0)
    for m in range(8):
        out_ref[pl.ds(m, DEVICES, stride=8), :] += acc_ref[m * LANES : (m + 1) * LANES, :].T


def partial_residual(table, received, head, integrals, coupling):
    whole = pl.BlockSpec(memory_space=pltpu.VMEM)
    hbm = pl.BlockSpec(memory_space=pltpu.HBM)
    return pl.pallas_call(
        main_kernel,
        out_shape=jax.ShapeDtypeStruct((DEVICES * 8, LANES), F32),
        in_specs=[hbm, whole, whole, hbm, whole],
        out_specs=whole,
        scratch_shapes=[
            pltpu.SMEM((SLOTS, 2, DEVICES), jnp.int32),
            pltpu.VMEM((SLOTS - 1, PAIR, PAIR), F32),
            pltpu.VMEM((SLOTS, 2 * DEVICES, PAIR), BF16),
            pltpu.VMEM((PAIR, DEVICES), F32),
            pltpu.VMEM((8, DEVICES, LANES), F32),
            pltpu.SemaphoreType.DMA((SLOTS + 1,)),
        ],
        compiler_params=pltpu.CompilerParams(vmem_limit_bytes=40 * 1024 * 1024),
        name="residual",
    )(
        pltpu.with_memory_space_constraint(table, pltpu.HBM),
        received,
        head,
        pltpu.with_memory_space_constraint(integrals, pltpu.HBM),
        coupling,
    )


def body(amplitudes, integrals, coupling, task_table):
    table = jnp.transpose(task_table, (1, 2, 0))
    outgoing, head = pack(table, amplitudes.reshape(V, V), integrals)
    received = lax.all_to_all(
        outgoing.reshape(DEVICES, MSG, 1, LANES), ROW_COL, split_axis=0, concat_axis=0, tiled=True
    ).reshape(DEVICES * MSG, LANES)
    partial = partial_residual(table, received, head, integrals, coupling.reshape(LANES, PAIR))
    terms = lax.all_to_all(partial.reshape(DEVICES, 8, LANES), ROW_COL, split_axis=0, concat_axis=0, tiled=True)
    return jnp.sum(terms, axis=0).reshape(1, PAIR)


def solution(mesh):
    split = Mesh(mesh.devices.reshape(4, 4, 4, 2), ("row_0", "row_1", "col_0", "col_1"))
    in_specs = (P(ROW_COL, None, None), P(ROW_COL, None, None), P(ROW_COL, None, None), P())
    return jax.shard_map(body, mesh=split, in_specs=in_specs, out_specs=P(ROW_COL, None), check_vma=False)
```

```python
import functools

import jax
import jax.numpy as jnp
from jax import lax
from jax.experimental import pallas as pl
from jax.experimental.pallas import tpu as pltpu
from jax.sharding import Mesh
from jax.sharding import PartitionSpec as P

TB = 32
NVT = 16
SLOTS = 4
DEVICES = 128
V = 512
PAIR = TB * TB
LANES = 128
MSG = SLOTS * 8 + 1
ROW_COL = ("row_0", "row_1", "col_0", "col_1")
F32 = jnp.float32
BF16 = jnp.bfloat16


def exchange_chunks(parts):
    lane = lax.broadcasted_iota(jnp.int32, parts[0].shape, parts[0].ndim - 1)
    odd = (lane // TB) % 2 == 1
    high = lane >= 2 * TB
    axis = parts[0].ndim - 1

    def swap(a, b, mask, shift):
        return (
            jnp.where(mask, pltpu.roll(b, shift, axis), a),
            jnp.where(mask, b, pltpu.roll(a, LANES - shift, axis)),
        )

    c0, c1 = swap(parts[0], parts[1], odd, TB)
    c2, c3 = swap(parts[2], parts[3], odd, TB)
    b0, b2 = swap(c0, c2, high, 2 * TB)
    b1, b3 = swap(c1, c3, high, 2 * TB)
    return b0, b1, b2, b3


QUARTERS = V // LANES
TILES = NVT * NVT


def pack_kernel(
    table_hbm, amp_hbm, int_hbm, send_ref, head_ref, table_ref, row_ref, place_ref, amp_ref, turned_ref, sems
):
    head_copy = pltpu.make_async_copy(int_hbm.at[0], head_ref, sems.at[QUARTERS + 1])
    table_copy = pltpu.make_async_copy(table_hbm, table_ref, sems.at[QUARTERS])
    table_copy.start()
    copies = []
    for group in range(QUARTERS):
        lanes = pl.ds(group * LANES, LANES)
        copies.append(pltpu.make_async_copy(amp_hbm.at[:, lanes], amp_ref.at[group], sems.at[group]))
        copies[-1].start()
    head_copy.start()
    table_copy.wait()
    sublane = lax.broadcasted_iota(jnp.int32, (8, DEVICES), 0)
    device = lax.broadcasted_iota(jnp.int32, (8, DEVICES), 1)
    tiles = lax.broadcasted_iota(jnp.int32, (TILES, DEVICES), 0)
    found = jnp.zeros((8, TILES), F32)
    for s in range(SLOTS):
        pair = table_ref[s, 0:1, :] * NVT + table_ref[s, 1:2, :]
        match = (tiles == pair).astype(F32).astype(BF16)
        found += nt_dot(jnp.where(sublane == 0, device, s).astype(F32).astype(BF16), match)
    row_ref[...] = (found[0:1] * MSG + found[1:2] * 8).astype(jnp.int32)
    row_copy = pltpu.make_async_copy(row_ref, place_ref, sems.at[QUARTERS])
    row_copy.start()
    copies[0].wait()
    row_copy.wait()
    for group in range(QUARTERS):
        if group:
            copies[group].wait()
        parts = [amp_ref[group, pl.ds(k, DEVICES, stride=4), :] for k in range(4)]
        for h, tiles in enumerate(exchange_chunks(parts)):
            for upper in range(NVT):
                row = place_ref[0, upper * NVT + group * 4 + h]
                send_ref[pl.ds(row, 8), :] = tiles[upper * 8 : (upper + 1) * 8]
        turned_ref[pl.ds(group * LANES, LANES), 0:TB] = amp_ref[group, 0:TB, :].T
    parts = [turned_ref[pl.ds(k, DEVICES, stride=4), :] for k in range(4)]
    send_ref[pl.ds(SLOTS * 8, DEVICES, stride=MSG), :] = exchange_chunks(parts)[0]
    head_copy.wait()


def pack(table, amplitudes, integrals):
    hbm = pl.BlockSpec(memory_space=pltpu.HBM)
    return pl.pallas_call(
        pack_kernel,
        out_shape=(
            jax.ShapeDtypeStruct((DEVICES * MSG, LANES), F32),
            jax.ShapeDtypeStruct((PAIR, PAIR), F32),
        ),
        in_specs=[hbm, hbm, hbm],
        out_specs=(pl.BlockSpec(memory_space=pltpu.VMEM),) * 2,
        scratch_shapes=[
            pltpu.VMEM((SLOTS, 2, DEVICES), jnp.int32),
            pltpu.VMEM((1, TILES), jnp.int32),
            pltpu.SMEM((1, TILES), jnp.int32),
            pltpu.VMEM((QUARTERS, V, LANES), F32),
            pltpu.VMEM((V, LANES), F32),
            pltpu.SemaphoreType.DMA((QUARTERS + 2,)),
        ],
        compiler_params=pltpu.CompilerParams(vmem_limit_bytes=16 * 1024 * 1024),
        name="pack",
    )(
        pltpu.with_memory_space_constraint(table, pltpu.HBM),
        pltpu.with_memory_space_constraint(amplitudes, pltpu.HBM),
        pltpu.with_memory_space_constraint(integrals, pltpu.HBM),
    )


def nt_dot(a, b):
    return lax.dot_general(a, b, (((1,), (1,)), ((), ())), preferred_element_type=F32)


def nn_dot(a, b):
    return lax.dot_general(a, b, (((1,), (0,)), ((), ())), preferred_element_type=F32)


def split_parts(value):
    high = value.astype(BF16)
    return high, (value - high.astype(F32)).astype(BF16)


PIECE = 256
HALF = DEVICES // 2


def main_kernel(
    table_hbm,
    recv_ref,
    head_ref,
    int_hbm,
    coup_ref,
    own_ref,
    other_ref,
    table_ref,
    int_ref,
    both_ref,
    acc_ref,
    hole_ref,
    turned_ref,
    sems,
):
    table_copy = pltpu.make_async_copy(table_hbm, table_ref, sems.at[SLOTS])
    table_copy.start()

    def fetch(slot):
        return pltpu.make_async_copy(int_hbm.at[slot], int_ref.at[slot - 1], sems.at[slot])

    fetch(1).start()
    core = lax.axis_index("col_1")

    def prepare(slot):
        for m in range(8):
            lanes = slice(m * LANES, (m + 1) * LANES)
            for half, parity in enumerate((core, 1 - core)):
                part = recv_ref[pl.ds(parity * MSG + slot * 8 + m, HALF, stride=2 * MSG), :]
                high, low = split_parts(part)
                both_ref[slot, half * HALF : (half + 1) * HALF, lanes] = high
                both_ref[slot, DEVICES + half * HALF : DEVICES + (half + 1) * HALF, lanes] = low

    def product(slot, values):
        int_high, int_low = split_parts(values)
        top = nt_dot(int_high, both_ref[slot])
        low = nt_dot(int_low, both_ref[slot, 0:DEVICES, :])
        return top[:, :DEVICES] + top[:, DEVICES:] + low

    pieces = [slice(first, first + PIECE) for first in range(0, PAIR, PIECE)]
    prepare(0)
    table_copy.wait()
    own = lax.axis_index(ROW_COL)
    count = jnp.int32(0)
    for s in range(SLOTS):
        count += (table_ref[s, 0, own] >= 0).astype(jnp.int32)
    for slot in range(2, SLOTS):

        @pl.when(slot < count)
        def _():
            fetch(slot).start()

    data = recv_ref[pl.ds(SLOTS * 8, DEVICES, stride=MSG), :]
    blocks = exchange_chunks([data[i * TB : (i + 1) * TB] for i in range(4)])
    left_high, left_low = split_parts(jnp.concatenate(blocks, axis=0).T)
    right_high, right_low = split_parts(coup_ref[...])
    hole = nn_dot(left_high, right_high) + nn_dot(left_low, right_high) + nn_dot(left_high, right_low)
    for group in range(8):
        hole_ref[group] = hole[:, group * LANES : (group + 1) * LANES]
    for group in range(8):
        parts = [hole_ref[group, pl.ds(k, DEVICES // 4, stride=4), :] for k in range(4)]
        for h, tiles in enumerate(exchange_chunks(parts)):
            for i in range(4):
                row = (i * TB + group * 4 + h) // 2 * 8
                half = h % 2 + core - 2 * (h % 2) * core
                turned_ref[pl.ds(half * (HALF * 8) + row, 8), :] = tiles[i * 8 : (i + 1) * 8]

    for rows in pieces:
        acc_ref[rows, :] = jnp.where(count > 0, product(0, head_ref[rows, :]), 0.0)
    fetch(1).wait()

    def add_slot(slot, _):
        prepare(slot)

        @pl.when(slot > 1)
        def _():
            fetch(slot).wait()

        for rows in pieces:
            acc_ref[rows, :] += product(slot, int_ref[slot - 1, rows, :])
        return 0

    lax.fori_loop(1, count, add_slot, 0)
    for m in range(8):
        ladder = acc_ref[m * LANES : (m + 1) * LANES, :].T
        for half, out_ref in enumerate((own_ref, other_ref)):
            hole = turned_ref[pl.ds(half * (HALF * 8) + m, HALF, stride=8), :]
            out_ref[pl.ds(m, HALF, stride=8), :] = hole + ladder[half * HALF : (half + 1) * HALF]


def partial_residual(table, received, head, integrals, coupling):
    whole = pl.BlockSpec(memory_space=pltpu.VMEM)
    hbm = pl.BlockSpec(memory_space=pltpu.HBM)
    return pl.pallas_call(
        main_kernel,
        out_shape=(jax.ShapeDtypeStruct((HALF * 8, LANES), F32),) * 2,
        in_specs=[hbm, whole, whole, hbm, whole],
        out_specs=(whole, whole),
        scratch_shapes=[
            pltpu.SMEM((SLOTS, 2, DEVICES), jnp.int32),
            pltpu.VMEM((SLOTS - 1, PAIR, PAIR), F32),
            pltpu.VMEM((SLOTS, 2 * DEVICES, PAIR), BF16),
            pltpu.VMEM((PAIR, DEVICES), F32),
            pltpu.VMEM((8, DEVICES, LANES), F32),
            pltpu.VMEM((DEVICES * 8, LANES), F32),
            pltpu.SemaphoreType.DMA((SLOTS + 1,)),
        ],
        compiler_params=pltpu.CompilerParams(vmem_limit_bytes=40 * 1024 * 1024),
        name="residual",
    )(
        pltpu.with_memory_space_constraint(table, pltpu.HBM),
        received,
        head,
        pltpu.with_memory_space_constraint(integrals, pltpu.HBM),
        coupling,
    )


def body(amplitudes, integrals, coupling, task_table):
    table = jnp.transpose(task_table, (1, 2, 0))
    outgoing, head = pack(table, amplitudes.reshape(V, V), integrals)
    received = lax.all_to_all(
        outgoing.reshape(DEVICES, MSG, 1, LANES), ROW_COL, split_axis=0, concat_axis=0, tiled=True
    ).reshape(DEVICES * MSG, LANES)
    own, other = partial_residual(table, received, head, integrals, coupling.reshape(LANES, PAIR))
    arrived = lax.ppermute(other, "col_1", [(0, 1), (1, 0)])
    chip = (own + arrived).reshape(HALF, 8, LANES)
    terms = lax.all_to_all(chip, ROW_COL[:3], split_axis=0, concat_axis=0, tiled=True)
    return jnp.sum(terms, axis=0).reshape(1, PAIR)


def solution(mesh):
    split = Mesh(mesh.devices.reshape(4, 4, 4, 2), ("row_0", "row_1", "col_0", "col_1"))
    in_specs = (P(ROW_COL, None, None), P(ROW_COL, None, None), P(ROW_COL, None, None), P())
    return jax.shard_map(body, mesh=split, in_specs=in_specs, out_specs=P(ROW_COL, None), check_vma=False)
```

```python
import functools

import jax
import jax.numpy as jnp
from jax import lax
from jax.experimental import pallas as pl
from jax.experimental.pallas import tpu as pltpu
from jax.sharding import Mesh
from jax.sharding import PartitionSpec as P

TB = 32
NVT = 16
SLOTS = 4
DEVICES = 128
V = 512
PAIR = TB * TB
LANES = 128
MSG = SLOTS * 8 + 1
ROW_COL = ("row_0", "row_1", "col_0", "col_1")
F32 = jnp.float32
BF16 = jnp.bfloat16


def exchange_chunks(parts):
    lane = lax.broadcasted_iota(jnp.int32, parts[0].shape, parts[0].ndim - 1)
    odd = (lane // TB) % 2 == 1
    high = lane >= 2 * TB
    axis = parts[0].ndim - 1

    def swap(a, b):
        return (
            jnp.where(odd, pltpu.roll(b, TB, axis), a),
            jnp.where(odd, b, pltpu.roll(a, LANES - TB, axis)),
        )

    def swap_halves(a, b):
        moved = pltpu.roll(jnp.where(high, a, b), 2 * TB, axis)
        return jnp.where(high, moved, a), jnp.where(high, b, moved)

    c0, c1 = swap(parts[0], parts[1])
    c2, c3 = swap(parts[2], parts[3])
    b0, b2 = swap_halves(c0, c2)
    b1, b3 = swap_halves(c1, c3)
    return b0, b1, b2, b3


QUARTERS = V // LANES
TILES = NVT * NVT
EXTRA = 256


def pack_kernel(
    table_hbm, amp_hbm, int_hbm, send_ref, head_ref, table_ref, row_ref, place_ref, amp_ref, turned_ref, sems
):
    head_copies = [
        pltpu.make_async_copy(int_hbm.at[0], head_ref.at[0:PAIR, :], sems.at[QUARTERS + 1]),
        pltpu.make_async_copy(int_hbm.at[1, 0:EXTRA, :], head_ref.at[PAIR:, :], sems.at[QUARTERS + 2]),
    ]
    table_copy = pltpu.make_async_copy(table_hbm, table_ref, sems.at[QUARTERS])
    table_copy.start()
    copies = []
    for group in range(QUARTERS):
        lanes = pl.ds(group * LANES, LANES)
        copies.append(pltpu.make_async_copy(amp_hbm.at[:, lanes], amp_ref.at[group], sems.at[group]))
        copies[-1].start()
    for copy in head_copies:
        copy.start()
    table_copy.wait()
    sublane = lax.broadcasted_iota(jnp.int32, (8, DEVICES), 0)
    device = lax.broadcasted_iota(jnp.int32, (8, DEVICES), 1)
    tiles = lax.broadcasted_iota(jnp.int32, (TILES, DEVICES), 0)
    found = jnp.zeros((8, TILES), F32)
    for s in range(SLOTS):
        pair = table_ref[s, 0:1, :] * NVT + table_ref[s, 1:2, :]
        match = (tiles == pair).astype(F32).astype(BF16)
        found += nt_dot(jnp.where(sublane == 0, device, s).astype(F32).astype(BF16), match)
    row_ref[...] = (found[0:1] * MSG + found[1:2] * 8).astype(jnp.int32)
    row_copy = pltpu.make_async_copy(row_ref, place_ref, sems.at[QUARTERS])
    row_copy.start()
    copies[0].wait()
    row_copy.wait()
    for group in range(QUARTERS):
        if group:
            copies[group].wait()
        parts = [amp_ref[group, pl.ds(k, DEVICES, stride=4), :] for k in range(4)]
        for h, tiles in enumerate(exchange_chunks(parts)):
            for upper in range(NVT):
                row = place_ref[0, upper * NVT + group * 4 + h]
                send_ref[pl.ds(row, 8), :] = tiles[upper * 8 : (upper + 1) * 8]
        turned_ref[pl.ds(group * LANES, LANES), 0:TB] = amp_ref[group, 0:TB, :].T
    parts = [turned_ref[pl.ds(k, DEVICES, stride=4), :] for k in range(4)]
    send_ref[pl.ds(SLOTS * 8, DEVICES, stride=MSG), :] = exchange_chunks(parts)[0]
    for copy in head_copies:
        copy.wait()


def pack(table, amplitudes, integrals):
    hbm = pl.BlockSpec(memory_space=pltpu.HBM)
    return pl.pallas_call(
        pack_kernel,
        out_shape=(
            jax.ShapeDtypeStruct((DEVICES * MSG, LANES), F32),
            jax.ShapeDtypeStruct((PAIR + EXTRA, PAIR), F32),
        ),
        in_specs=[hbm, hbm, hbm],
        out_specs=(pl.BlockSpec(memory_space=pltpu.VMEM),) * 2,
        scratch_shapes=[
            pltpu.VMEM((SLOTS, 2, DEVICES), jnp.int32),
            pltpu.VMEM((1, TILES), jnp.int32),
            pltpu.SMEM((1, TILES), jnp.int32),
            pltpu.VMEM((QUARTERS, V, LANES), F32),
            pltpu.VMEM((V, LANES), F32),
            pltpu.SemaphoreType.DMA((QUARTERS + 3,)),
        ],
        compiler_params=pltpu.CompilerParams(vmem_limit_bytes=16 * 1024 * 1024),
        name="pack",
    )(
        pltpu.with_memory_space_constraint(table, pltpu.HBM),
        pltpu.with_memory_space_constraint(amplitudes, pltpu.HBM),
        pltpu.with_memory_space_constraint(integrals, pltpu.HBM),
    )


def nt_dot(a, b):
    return lax.dot_general(a, b, (((1,), (1,)), ((), ())), preferred_element_type=F32)


def nn_dot(a, b):
    return lax.dot_general(a, b, (((1,), (0,)), ((), ())), preferred_element_type=F32)


def split_parts(value):
    high = value.astype(BF16)
    return high, (value - high.astype(F32)).astype(BF16)


PIECE = 256
HALF = DEVICES // 2


def main_kernel(
    table_hbm,
    recv_ref,
    head_ref,
    int_hbm,
    coup_ref,
    own_ref,
    other_ref,
    table_ref,
    int_ref,
    both_ref,
    acc_ref,
    hole_ref,
    turned_ref,
    sems,
):
    table_copy = pltpu.make_async_copy(table_hbm, table_ref, sems.at[SLOTS])
    table_copy.start()

    def fetch(slot):
        rows = pl.ds(EXTRA, PAIR - EXTRA) if slot == 1 else pl.ds(0, PAIR)
        return pltpu.make_async_copy(int_hbm.at[slot, rows, :], int_ref.at[slot - 1, rows, :], sems.at[slot])

    fetch(1).start()
    core = lax.axis_index("col_1")

    def prepare(slot):
        for m in range(8):
            lanes = slice(m * LANES, (m + 1) * LANES)
            for half, parity in enumerate((core, 1 - core)):
                part = recv_ref[pl.ds(parity * MSG + slot * 8 + m, HALF, stride=2 * MSG), :]
                high, low = split_parts(part)
                both_ref[slot, half * HALF : (half + 1) * HALF, lanes] = high
                both_ref[slot, DEVICES + half * HALF : DEVICES + (half + 1) * HALF, lanes] = low

    def product(slot, values):
        int_high, int_low = split_parts(values)
        top = nt_dot(int_high, both_ref[slot])
        low = nt_dot(int_low, both_ref[slot, 0:DEVICES, :])
        return top[:, :DEVICES] + top[:, DEVICES:] + low

    pieces = [slice(first, first + PIECE) for first in range(0, PAIR, PIECE)]
    fetch(2).start()
    fetch(3).start()
    prepare(0)
    data = recv_ref[pl.ds(SLOTS * 8, DEVICES, stride=MSG), :]
    blocks = exchange_chunks([data[i * TB : (i + 1) * TB] for i in range(4)])
    left_high, left_low = split_parts(jnp.concatenate(blocks, axis=0).T)
    right_high, right_low = split_parts(coup_ref[...])
    hole = nn_dot(left_high, right_high) + nn_dot(left_low, right_high) + nn_dot(left_high, right_low)
    for group in range(8):
        hole_ref[group] = hole[:, group * LANES : (group + 1) * LANES]
    for group in range(8):
        parts = [hole_ref[group, pl.ds(k, DEVICES // 4, stride=4), :] for k in range(4)]
        for h, tiles in enumerate(exchange_chunks(parts)):
            for i in range(4):
                row = (i * TB + group * 4 + h) // 2 * 8
                half = h % 2 + core - 2 * (h % 2) * core
                turned_ref[pl.ds(half * (HALF * 8) + row, 8), :] = tiles[i * 8 : (i + 1) * 8]

    for rows in pieces:
        acc_ref[rows, :] = product(0, head_ref[rows, :])
    table_copy.wait()
    own = lax.axis_index(ROW_COL)
    count = jnp.int32(0)
    for s in range(SLOTS):
        count += (table_ref[s, 0, own] >= 0).astype(jnp.int32)
    for rows in pieces:
        acc_ref[rows, :] = jnp.where(count > 0, acc_ref[rows, :], 0.0)
    for slot in range(1, SLOTS):
        prepare(slot)
        fetch(slot).wait()
        for rows in pieces:
            early = slot == 1 and rows.start < EXTRA
            values = head_ref[PAIR + rows.start : PAIR + rows.stop, :] if early else int_ref[slot - 1, rows, :]
            term = product(slot, values)
            acc_ref[rows, :] += jnp.where(count > slot, term, 0.0)
    for m in range(8):
        ladder = acc_ref[m * LANES : (m + 1) * LANES, :].T
        for half, out_ref in enumerate((own_ref, other_ref)):
            hole = turned_ref[pl.ds(half * (HALF * 8) + m, HALF, stride=8), :]
            out_ref[pl.ds(m, HALF, stride=8), :] = hole + ladder[half * HALF : (half + 1) * HALF]


def partial_residual(table, received, head, integrals, coupling):
    whole = pl.BlockSpec(memory_space=pltpu.VMEM)
    hbm = pl.BlockSpec(memory_space=pltpu.HBM)
    return pl.pallas_call(
        main_kernel,
        out_shape=(jax.ShapeDtypeStruct((HALF * 8, LANES), F32),) * 2,
        in_specs=[hbm, whole, whole, hbm, whole],
        out_specs=(whole, whole),
        scratch_shapes=[
            pltpu.SMEM((SLOTS, 2, DEVICES), jnp.int32),
            pltpu.VMEM((SLOTS - 1, PAIR, PAIR), F32),
            pltpu.VMEM((SLOTS, 2 * DEVICES, PAIR), BF16),
            pltpu.VMEM((PAIR, DEVICES), F32),
            pltpu.VMEM((8, DEVICES, LANES), F32),
            pltpu.VMEM((DEVICES * 8, LANES), F32),
            pltpu.SemaphoreType.DMA((SLOTS + 1,)),
        ],
        compiler_params=pltpu.CompilerParams(vmem_limit_bytes=40 * 1024 * 1024),
        name="residual",
    )(
        pltpu.with_memory_space_constraint(table, pltpu.HBM),
        received,
        head,
        pltpu.with_memory_space_constraint(integrals, pltpu.HBM),
        coupling,
    )


def body(amplitudes, integrals, coupling, task_table):
    table = jnp.transpose(task_table, (1, 2, 0))
    outgoing, head = pack(table, amplitudes.reshape(V, V), integrals)
    received = lax.all_to_all(
        outgoing.reshape(DEVICES, MSG, 1, LANES), ROW_COL, split_axis=0, concat_axis=0, tiled=True
    ).reshape(DEVICES * MSG, LANES)
    own, other = partial_residual(table, received, head, integrals, coupling.reshape(LANES, PAIR))
    arrived = lax.ppermute(other, "col_1", [(0, 1), (1, 0)])
    chip = (own + arrived).reshape(HALF, 8, LANES)
    terms = lax.all_to_all(chip, ROW_COL[:3], split_axis=0, concat_axis=0, tiled=True)
    return jnp.sum(terms, axis=0).reshape(1, PAIR)


def solution(mesh):
    split = Mesh(mesh.devices.reshape(4, 4, 4, 2), ("row_0", "row_1", "col_0", "col_1"))
    in_specs = (P(ROW_COL, None, None), P(ROW_COL, None, None), P(ROW_COL, None, None), P())
    return jax.shard_map(body, mesh=split, in_specs=in_specs, out_specs=P(ROW_COL, None), check_vma=False)
```

```python
import functools

import jax
import jax.numpy as jnp
from jax import lax
from jax.experimental import pallas as pl
from jax.experimental.pallas import tpu as pltpu
from jax.sharding import Mesh
from jax.sharding import PartitionSpec as P

TB = 32
NVT = 16
SLOTS = 4
DEVICES = 128
V = 512
PAIR = TB * TB
LANES = 128
MSG = SLOTS * 8 + 1
ROW_COL = ("row_0", "row_1", "col_0", "col_1")
F32 = jnp.float32
BF16 = jnp.bfloat16


def exchange_chunks(parts):
    lane = lax.broadcasted_iota(jnp.int32, parts[0].shape, parts[0].ndim - 1)
    odd = (lane // TB) % 2 == 1
    high = lane >= 2 * TB
    axis = parts[0].ndim - 1

    def swap(a, b, mask, shift):
        return (
            jnp.where(mask, pltpu.roll(b, shift, axis), a),
            jnp.where(mask, b, pltpu.roll(a, LANES - shift, axis)),
        )

    c0, c1 = swap(parts[0], parts[1], odd, TB)
    c2, c3 = swap(parts[2], parts[3], odd, TB)
    b0, b2 = swap(c0, c2, high, 2 * TB)
    b1, b3 = swap(c1, c3, high, 2 * TB)
    return b0, b1, b2, b3


QUARTERS = V // LANES
TILES = NVT * NVT


def pack_kernel(
    table_hbm, amp_hbm, int_hbm, send_ref, head_ref, table_ref, row_ref, place_ref, first_ref, amp_ref, turned_ref, sems
):
    head_copy = pltpu.make_async_copy(int_hbm.at[0], head_ref, sems.at[QUARTERS + 1])
    table_copy = pltpu.make_async_copy(table_hbm, table_ref, sems.at[QUARTERS])
    table_copy.start()
    first_copy = pltpu.make_async_copy(amp_hbm.at[pl.ds(0, TB), :], first_ref, sems.at[QUARTERS + 2])
    first_copy.start()
    copies = []
    for group in range(QUARTERS):
        lanes = pl.ds(group * LANES, LANES)
        copies.append(pltpu.make_async_copy(amp_hbm.at[:, lanes], amp_ref.at[group], sems.at[group]))
        copies[-1].start()
    head_copy.start()
    table_copy.wait()
    sublane = lax.broadcasted_iota(jnp.int32, (8, DEVICES), 0)
    device = lax.broadcasted_iota(jnp.int32, (8, DEVICES), 1)
    tiles = lax.broadcasted_iota(jnp.int32, (TILES, DEVICES), 0)
    found = jnp.zeros((8, TILES), F32)
    for s in range(SLOTS):
        pair = table_ref[s, 0:1, :] * NVT + table_ref[s, 1:2, :]
        match = (tiles == pair).astype(F32).astype(BF16)
        found += nt_dot(jnp.where(sublane == 0, device, s).astype(F32).astype(BF16), match)
    row_ref[...] = (found[0:1] * MSG + found[1:2] * 8).astype(jnp.int32)
    row_copy = pltpu.make_async_copy(row_ref, place_ref, sems.at[QUARTERS])
    row_copy.start()
    first_copy.wait()
    for group in range(QUARTERS):
        lanes = slice(group * LANES, (group + 1) * LANES)
        turned_ref[lanes, 0:TB] = first_ref[:, lanes].T
    parts = [turned_ref[pl.ds(k, DEVICES, stride=4), :] for k in range(4)]
    send_ref[pl.ds(SLOTS * 8, DEVICES, stride=MSG), :] = exchange_chunks(parts)[0]
    copies[0].wait()
    row_copy.wait()
    for group in range(QUARTERS):
        if group:
            copies[group].wait()
        parts = [amp_ref[group, pl.ds(k, DEVICES, stride=4), :] for k in range(4)]
        for h, tiles in enumerate(exchange_chunks(parts)):
            for upper in range(NVT):
                row = place_ref[0, upper * NVT + group * 4 + h]
                send_ref[pl.ds(row, 8), :] = tiles[upper * 8 : (upper + 1) * 8]
    head_copy.wait()


def pack(table, amplitudes, integrals):
    hbm = pl.BlockSpec(memory_space=pltpu.HBM)
    return pl.pallas_call(
        pack_kernel,
        out_shape=(
            jax.ShapeDtypeStruct((DEVICES * MSG, LANES), F32),
            jax.ShapeDtypeStruct((PAIR, PAIR), F32),
        ),
        in_specs=[hbm, hbm, hbm],
        out_specs=(pl.BlockSpec(memory_space=pltpu.VMEM),) * 2,
        scratch_shapes=[
            pltpu.VMEM((SLOTS, 2, DEVICES), jnp.int32),
            pltpu.VMEM((1, TILES), jnp.int32),
            pltpu.SMEM((1, TILES), jnp.int32),
            pltpu.VMEM((TB, V), F32),
            pltpu.VMEM((QUARTERS, V, LANES), F32),
            pltpu.VMEM((V, LANES), F32),
            pltpu.SemaphoreType.DMA((QUARTERS + 3,)),
        ],
        compiler_params=pltpu.CompilerParams(vmem_limit_bytes=16 * 1024 * 1024),
        name="pack",
    )(
        pltpu.with_memory_space_constraint(table, pltpu.HBM),
        pltpu.with_memory_space_constraint(amplitudes, pltpu.HBM),
        pltpu.with_memory_space_constraint(integrals, pltpu.HBM),
    )


def nt_dot(a, b):
    return lax.dot_general(a, b, (((1,), (1,)), ((), ())), preferred_element_type=F32)


def nn_dot(a, b):
    return lax.dot_general(a, b, (((1,), (0,)), ((), ())), preferred_element_type=F32)


def split_parts(value):
    high = value.astype(BF16)
    return high, (value - high.astype(F32)).astype(BF16)


PIECE = 256
HALF = DEVICES // 2


def main_kernel(
    table_hbm,
    recv_ref,
    head_ref,
    int_hbm,
    coup_ref,
    own_ref,
    other_ref,
    table_ref,
    int_ref,
    both_ref,
    acc_ref,
    hole_ref,
    turned_ref,
    sems,
):
    table_copy = pltpu.make_async_copy(table_hbm, table_ref, sems.at[SLOTS])
    table_copy.start()

    def fetch(slot):
        return pltpu.make_async_copy(int_hbm.at[slot], int_ref.at[slot - 1], sems.at[slot])

    fetch(1).start()
    core = lax.axis_index("col_1")

    def prepare(slot):
        for m in range(8):
            lanes = slice(m * LANES, (m + 1) * LANES)
            for half, parity in enumerate((core, 1 - core)):
                part = recv_ref[pl.ds(parity * MSG + slot * 8 + m, HALF, stride=2 * MSG), :]
                high, low = split_parts(part)
                both_ref[slot, half * HALF : (half + 1) * HALF, lanes] = high
                both_ref[slot, DEVICES + half * HALF : DEVICES + (half + 1) * HALF, lanes] = low

    def product(slot, values):
        int_high, int_low = split_parts(values)
        top = nt_dot(int_high, both_ref[slot])
        low = nt_dot(int_low, both_ref[slot, 0:DEVICES, :])
        return top[:, :DEVICES] + top[:, DEVICES:] + low

    pieces = [slice(first, first + PIECE) for first in range(0, PAIR, PIECE)]
    fetch(2).start()
    fetch(3).start()
    prepare(0)
    data = recv_ref[pl.ds(SLOTS * 8, DEVICES, stride=MSG), :]
    blocks = exchange_chunks([data[i * TB : (i + 1) * TB] for i in range(4)])
    left_high, left_low = split_parts(jnp.concatenate(blocks, axis=0).T)
    right_high, right_low = split_parts(coup_ref[...])
    hole = nn_dot(left_high, right_high) + nn_dot(left_low, right_high) + nn_dot(left_high, right_low)
    for group in range(8):
        hole_ref[group] = hole[:, group * LANES : (group + 1) * LANES]
    for group in range(8):
        parts = [hole_ref[group, pl.ds(k, DEVICES // 4, stride=4), :] for k in range(4)]
        for h, tiles in enumerate(exchange_chunks(parts)):
            for i in range(4):
                row = (i * TB + group * 4 + h) // 2 * 8
                half = h % 2 + core - 2 * (h % 2) * core
                turned_ref[pl.ds(half * (HALF * 8) + row, 8), :] = tiles[i * 8 : (i + 1) * 8]

    for rows in pieces:
        acc_ref[rows, :] = product(0, head_ref[rows, :])
    table_copy.wait()
    own = lax.axis_index(ROW_COL)
    count = jnp.int32(0)
    for s in range(SLOTS):
        count += (table_ref[s, 0, own] >= 0).astype(jnp.int32)

    @pl.when(count == 0)
    def _():
        acc_ref[...] = jnp.zeros_like(acc_ref)

    fetch(1).wait()

    @pl.when(count > 1)
    def _():
        prepare(1)
        for rows in pieces:
            acc_ref[rows, :] += product(1, int_ref[1 - 1, rows, :])

    fetch(2).wait()

    @pl.when(count > 2)
    def _():
        prepare(2)
        for rows in pieces:
            acc_ref[rows, :] += product(2, int_ref[2 - 1, rows, :])

    fetch(3).wait()

    @pl.when(count > 3)
    def _():
        prepare(3)
        for rows in pieces:
            acc_ref[rows, :] += product(3, int_ref[3 - 1, rows, :])

    for m in range(8):
        ladder = acc_ref[m * LANES : (m + 1) * LANES, :].T
        for half, out_ref in enumerate((own_ref, other_ref)):
            hole = turned_ref[pl.ds(half * (HALF * 8) + m, HALF, stride=8), :]
            out_ref[pl.ds(m, HALF, stride=8), :] = hole + ladder[half * HALF : (half + 1) * HALF]


def partial_residual(table, received, head, integrals, coupling):
    whole = pl.BlockSpec(memory_space=pltpu.VMEM)
    hbm = pl.BlockSpec(memory_space=pltpu.HBM)
    return pl.pallas_call(
        main_kernel,
        out_shape=(jax.ShapeDtypeStruct((HALF * 8, LANES), F32),) * 2,
        in_specs=[hbm, whole, whole, hbm, whole],
        out_specs=(whole, whole),
        scratch_shapes=[
            pltpu.SMEM((SLOTS, 2, DEVICES), jnp.int32),
            pltpu.VMEM((SLOTS - 1, PAIR, PAIR), F32),
            pltpu.VMEM((SLOTS, 2 * DEVICES, PAIR), BF16),
            pltpu.VMEM((PAIR, DEVICES), F32),
            pltpu.VMEM((8, DEVICES, LANES), F32),
            pltpu.VMEM((DEVICES * 8, LANES), F32),
            pltpu.SemaphoreType.DMA((SLOTS + 1,)),
        ],
        compiler_params=pltpu.CompilerParams(vmem_limit_bytes=40 * 1024 * 1024),
        name="residual",
    )(
        pltpu.with_memory_space_constraint(table, pltpu.HBM),
        received,
        head,
        pltpu.with_memory_space_constraint(integrals, pltpu.HBM),
        coupling,
    )


def body(amplitudes, integrals, coupling, task_table):
    table = jnp.transpose(task_table, (1, 2, 0))
    outgoing, head = pack(table, amplitudes.reshape(V, V), integrals)
    received = lax.all_to_all(
        outgoing.reshape(DEVICES, MSG, 1, LANES), ROW_COL, split_axis=0, concat_axis=0, tiled=True
    ).reshape(DEVICES * MSG, LANES)
    own, other = partial_residual(table, received, head, integrals, coupling.reshape(LANES, PAIR))
    arrived = lax.ppermute(other, "col_1", [(0, 1), (1, 0)])
    chip = (own + arrived).reshape(HALF, 8, LANES)
    terms = lax.all_to_all(chip, ROW_COL[:3], split_axis=0, concat_axis=0, tiled=True)
    return jnp.sum(terms, axis=0).reshape(1, PAIR)


def solution(mesh):
    split = Mesh(mesh.devices.reshape(4, 4, 4, 2), ("row_0", "row_1", "col_0", "col_1"))
    in_specs = (P(ROW_COL, None, None), P(ROW_COL, None, None), P(ROW_COL, None, None), P())
    return jax.shard_map(body, mesh=split, in_specs=in_specs, out_specs=P(ROW_COL, None), check_vma=False)
```

```python
import functools

import jax
import jax.numpy as jnp
from jax import lax
from jax.experimental import pallas as pl
from jax.experimental.pallas import tpu as pltpu
from jax.sharding import Mesh
from jax.sharding import PartitionSpec as P

TB = 32
NVT = 16
SLOTS = 4
DEVICES = 128
V = 512
PAIR = TB * TB
LANES = 128
MSG = SLOTS * 8 + 1
ROW_COL = ("row_0", "row_1", "col_0", "col_1")
F32 = jnp.float32
BF16 = jnp.bfloat16


def exchange_chunks(parts):
    lane = lax.broadcasted_iota(jnp.int32, parts[0].shape, parts[0].ndim - 1)
    odd = (lane // TB) % 2 == 1
    high = lane >= 2 * TB
    axis = parts[0].ndim - 1

    def swap(a, b, mask, shift):
        return (
            jnp.where(mask, pltpu.roll(b, shift, axis), a),
            jnp.where(mask, b, pltpu.roll(a, LANES - shift, axis)),
        )

    c0, c1 = swap(parts[0], parts[1], odd, TB)
    c2, c3 = swap(parts[2], parts[3], odd, TB)
    b0, b2 = swap(c0, c2, high, 2 * TB)
    b1, b3 = swap(c1, c3, high, 2 * TB)
    return b0, b1, b2, b3


QUARTERS = V // LANES
TILES = NVT * NVT


def pack_kernel(
    table_hbm, amp_hbm, int_hbm, send_ref, head_ref, table_ref, row_ref, place_ref, first_ref, amp_ref, turned_ref, sems
):
    head_copy = pltpu.make_async_copy(int_hbm.at[0], head_ref, sems.at[QUARTERS + 1])
    table_copy = pltpu.make_async_copy(table_hbm, table_ref, sems.at[QUARTERS])
    table_copy.start()
    first_copy = pltpu.make_async_copy(amp_hbm.at[pl.ds(0, TB), :], first_ref, sems.at[QUARTERS + 2])
    first_copy.start()
    copies = []
    for group in range(QUARTERS):
        lanes = pl.ds(group * LANES, LANES)
        copies.append(pltpu.make_async_copy(amp_hbm.at[:, lanes], amp_ref.at[group], sems.at[group]))
        copies[-1].start()
    head_copy.start()
    table_copy.wait()
    sublane = lax.broadcasted_iota(jnp.int32, (8, DEVICES), 0)
    device = lax.broadcasted_iota(jnp.int32, (8, DEVICES), 1)
    tiles = lax.broadcasted_iota(jnp.int32, (TILES, DEVICES), 0)
    found = jnp.zeros((8, TILES), F32)
    for s in range(SLOTS):
        pair = table_ref[s, 0:1, :] * NVT + table_ref[s, 1:2, :]
        match = (tiles == pair).astype(F32).astype(BF16)
        found += nt_dot(jnp.where(sublane == 0, device, s).astype(F32).astype(BF16), match)
    row_ref[...] = (found[0:1] * MSG + found[1:2] * 8).astype(jnp.int32)
    row_copy = pltpu.make_async_copy(row_ref, place_ref, sems.at[QUARTERS])
    row_copy.start()
    first_copy.wait()
    for group in range(QUARTERS):
        lanes = slice(group * LANES, (group + 1) * LANES)
        turned_ref[lanes, 0:TB] = first_ref[:, lanes].T
    parts = [turned_ref[pl.ds(k, DEVICES, stride=4), :] for k in range(4)]
    send_ref[pl.ds(SLOTS * 8, DEVICES, stride=MSG), :] = exchange_chunks(parts)[0]
    copies[0].wait()
    row_copy.wait()
    for group in range(QUARTERS):
        if group:
            copies[group].wait()
        parts = [amp_ref[group, pl.ds(k, DEVICES, stride=4), :] for k in range(4)]
        for h, tiles in enumerate(exchange_chunks(parts)):
            for upper in range(NVT):
                row = place_ref[0, upper * NVT + group * 4 + h]
                send_ref[pl.ds(row, 8), :] = tiles[upper * 8 : (upper + 1) * 8]
    head_copy.wait()


def pack(table, amplitudes, integrals):
    hbm = pl.BlockSpec(memory_space=pltpu.HBM)
    return pl.pallas_call(
        pack_kernel,
        out_shape=(
            jax.ShapeDtypeStruct((DEVICES * MSG, LANES), F32),
            jax.ShapeDtypeStruct((PAIR, PAIR), F32),
        ),
        in_specs=[hbm, hbm, hbm],
        out_specs=(pl.BlockSpec(memory_space=pltpu.VMEM),) * 2,
        scratch_shapes=[
            pltpu.VMEM((SLOTS, 2, DEVICES), jnp.int32),
            pltpu.VMEM((1, TILES), jnp.int32),
            pltpu.SMEM((1, TILES), jnp.int32),
            pltpu.VMEM((TB, V), F32),
            pltpu.VMEM((QUARTERS, V, LANES), F32),
            pltpu.VMEM((V, LANES), F32),
            pltpu.SemaphoreType.DMA((QUARTERS + 3,)),
        ],
        compiler_params=pltpu.CompilerParams(vmem_limit_bytes=16 * 1024 * 1024),
        name="pack",
    )(
        pltpu.with_memory_space_constraint(table, pltpu.HBM),
        pltpu.with_memory_space_constraint(amplitudes, pltpu.HBM),
        pltpu.with_memory_space_constraint(integrals, pltpu.HBM),
    )


def nt_dot(a, b):
    return lax.dot_general(a, b, (((1,), (1,)), ((), ())), preferred_element_type=F32)


def nn_dot(a, b):
    return lax.dot_general(a, b, (((1,), (0,)), ((), ())), preferred_element_type=F32)


def split_parts(value):
    high = value.astype(BF16)
    return high, (value - high.astype(F32)).astype(BF16)


PIECE = 256
HALF = DEVICES // 2


def main_kernel(
    table_hbm,
    recv_ref,
    head_ref,
    int_hbm,
    coup_ref,
    own_ref,
    other_ref,
    table_ref,
    int_ref,
    both_ref,
    acc_ref,
    hole_ref,
    turned_ref,
    sems,
):
    table_copy = pltpu.make_async_copy(table_hbm, table_ref, sems.at[SLOTS])
    table_copy.start()

    def fetch(slot):
        return pltpu.make_async_copy(int_hbm.at[slot], int_ref.at[slot - 1], sems.at[slot])

    fetch(1).start()
    core = lax.axis_index("col_1")

    def prepare(slot):
        for m in range(8):
            lanes = slice(m * LANES, (m + 1) * LANES)
            for half, parity in enumerate((core, 1 - core)):
                part = recv_ref[pl.ds(parity * MSG + slot * 8 + m, HALF, stride=2 * MSG), :]
                high, low = split_parts(part)
                both_ref[slot, half * HALF : (half + 1) * HALF, lanes] = high
                both_ref[slot, DEVICES + half * HALF : DEVICES + (half + 1) * HALF, lanes] = low

    def product(slot, values):
        int_high, int_low = split_parts(values)
        top = nt_dot(int_high, both_ref[slot])
        low = nt_dot(int_low, both_ref[slot, 0:DEVICES, :])
        return top[:, :DEVICES] + top[:, DEVICES:] + low

    pieces = [slice(first, first + PIECE) for first in range(0, PAIR, PIECE)]
    prepare(0)
    table_copy.wait()
    own = lax.axis_index(ROW_COL)
    count = jnp.int32(0)
    for s in range(SLOTS):
        count += (table_ref[s, 0, own] >= 0).astype(jnp.int32)
    for slot in range(2, SLOTS):

        @pl.when(slot < count)
        def _():
            fetch(slot).start()

    data = recv_ref[pl.ds(SLOTS * 8, DEVICES, stride=MSG), :]
    blocks = exchange_chunks([data[i * TB : (i + 1) * TB] for i in range(4)])
    left_high, left_low = split_parts(jnp.concatenate(blocks, axis=0).T)
    right_high, right_low = split_parts(coup_ref[...])
    hole = nn_dot(left_high, right_high) + nn_dot(left_low, right_high) + nn_dot(left_high, right_low)
    for group in range(8):
        hole_ref[group] = hole[:, group * LANES : (group + 1) * LANES]
    for group in range(8):
        parts = [hole_ref[group, pl.ds(k, DEVICES // 4, stride=4), :] for k in range(4)]
        for h, tiles in enumerate(exchange_chunks(parts)):
            for i in range(4):
                row = (i * TB + group * 4 + h) // 2 * 8
                half = h % 2 + core - 2 * (h % 2) * core
                turned_ref[pl.ds(half * (HALF * 8) + row, 8), :] = tiles[i * 8 : (i + 1) * 8]

    for rows in pieces:
        acc_ref[rows, :] = jnp.where(count > 0, product(0, head_ref[rows, :]), 0.0)
    fetch(1).wait()

    def add_slot(slot, _):
        prepare(slot)

        @pl.when(slot > 1)
        def _():
            fetch(slot).wait()

        for rows in pieces:
            acc_ref[rows, :] += product(slot, int_ref[slot - 1, rows, :])
        return 0

    lax.fori_loop(1, count, add_slot, 0)
    for m in range(8):
        ladder = acc_ref[m * LANES : (m + 1) * LANES, :].T
        for half, out_ref in enumerate((own_ref, other_ref)):
            hole = turned_ref[pl.ds(half * (HALF * 8) + m, HALF, stride=8), :]
            out_ref[pl.ds(m, HALF, stride=8), :] = hole + ladder[half * HALF : (half + 1) * HALF]


def partial_residual(table, received, head, integrals, coupling):
    whole = pl.BlockSpec(memory_space=pltpu.VMEM)
    hbm = pl.BlockSpec(memory_space=pltpu.HBM)
    return pl.pallas_call(
        main_kernel,
        out_shape=(jax.ShapeDtypeStruct((HALF * 8, LANES), F32),) * 2,
        in_specs=[hbm, whole, whole, hbm, whole],
        out_specs=(whole, whole),
        scratch_shapes=[
            pltpu.SMEM((SLOTS, 2, DEVICES), jnp.int32),
            pltpu.VMEM((SLOTS - 1, PAIR, PAIR), F32),
            pltpu.VMEM((SLOTS, 2 * DEVICES, PAIR), BF16),
            pltpu.VMEM((PAIR, DEVICES), F32),
            pltpu.VMEM((8, DEVICES, LANES), F32),
            pltpu.VMEM((DEVICES * 8, LANES), F32),
            pltpu.SemaphoreType.DMA((SLOTS + 1,)),
        ],
        compiler_params=pltpu.CompilerParams(vmem_limit_bytes=40 * 1024 * 1024),
        name="residual",
    )(
        pltpu.with_memory_space_constraint(table, pltpu.HBM),
        received,
        head,
        pltpu.with_memory_space_constraint(integrals, pltpu.HBM),
        coupling,
    )


def body(amplitudes, integrals, coupling, task_table):
    table = jnp.transpose(task_table, (1, 2, 0))
    outgoing, head = pack(table, amplitudes.reshape(V, V), integrals)
    received = lax.all_to_all(
        outgoing.reshape(DEVICES, MSG, 1, LANES), ROW_COL, split_axis=0, concat_axis=0, tiled=True
    ).reshape(DEVICES * MSG, LANES)
    own, other = partial_residual(table, received, head, integrals, coupling.reshape(LANES, PAIR))
    arrived = lax.ppermute(other, "col_1", [(0, 1), (1, 0)])
    chip = (own + arrived).reshape(HALF, 8, LANES)
    terms = lax.all_to_all(chip, ROW_COL[:3], split_axis=0, concat_axis=0, tiled=True)
    return jnp.sum(terms, axis=0).reshape(1, PAIR)


def solution(mesh):
    split = Mesh(mesh.devices.reshape(4, 4, 4, 2), ("row_0", "row_1", "col_0", "col_1"))
    in_specs = (P(ROW_COL, None, None), P(ROW_COL, None, None), P(ROW_COL, None, None), P())
    return jax.shard_map(body, mesh=split, in_specs=in_specs, out_specs=P(ROW_COL, None), check_vma=False)
```

```python
import functools

import jax
import jax.numpy as jnp
from jax import lax
from jax.experimental import pallas as pl
from jax.experimental.pallas import tpu as pltpu
from jax.sharding import Mesh
from jax.sharding import PartitionSpec as P

TB = 32
NVT = 16
SLOTS = 4
DEVICES = 128
V = 512
PAIR = TB * TB
LANES = 128
MSG = SLOTS * 8 + 1
ROW_COL = ("row_0", "row_1", "col_0", "col_1")
F32 = jnp.float32
BF16 = jnp.bfloat16


def exchange_chunks(parts):
    lane = lax.broadcasted_iota(jnp.int32, parts[0].shape, parts[0].ndim - 1)
    odd = (lane // TB) % 2 == 1
    high = lane >= 2 * TB
    axis = parts[0].ndim - 1

    def swap(a, b, mask, shift):
        return (
            jnp.where(mask, pltpu.roll(b, shift, axis), a),
            jnp.where(mask, b, pltpu.roll(a, LANES - shift, axis)),
        )

    c0, c1 = swap(parts[0], parts[1], odd, TB)
    c2, c3 = swap(parts[2], parts[3], odd, TB)
    b0, b2 = swap(c0, c2, high, 2 * TB)
    b1, b3 = swap(c1, c3, high, 2 * TB)
    return b0, b1, b2, b3


QUARTERS = V // LANES
TILES = NVT * NVT


def pack_kernel(
    table_hbm, amp_hbm, int_hbm, send_ref, head_ref, table_ref, row_ref, place_ref, first_ref, amp_ref, turned_ref, sems
):
    head_copy = pltpu.make_async_copy(int_hbm.at[0], head_ref, sems.at[QUARTERS + 1])
    table_copy = pltpu.make_async_copy(table_hbm, table_ref, sems.at[QUARTERS])
    table_copy.start()
    first_copy = pltpu.make_async_copy(amp_hbm.at[pl.ds(0, TB), :], first_ref, sems.at[QUARTERS + 2])
    first_copy.start()
    copies = []
    for group in range(QUARTERS):
        lanes = pl.ds(group * LANES, LANES)
        copies.append(pltpu.make_async_copy(amp_hbm.at[:, lanes], amp_ref.at[group], sems.at[group]))
        copies[-1].start()
    head_copy.start()
    table_copy.wait()
    sublane = lax.broadcasted_iota(jnp.int32, (8, DEVICES), 0)
    device = lax.broadcasted_iota(jnp.int32, (8, DEVICES), 1)
    tiles = lax.broadcasted_iota(jnp.int32, (TILES, DEVICES), 0)
    found = jnp.zeros((8, TILES), F32)
    for s in range(SLOTS):
        pair = table_ref[s, 0:1, :] * NVT + table_ref[s, 1:2, :]
        match = (tiles == pair).astype(F32).astype(BF16)
        found += nt_dot(jnp.where(sublane == 0, device, s).astype(F32).astype(BF16), match)
    row_ref[...] = (found[0:1] * MSG + found[1:2] * 8).astype(jnp.int32)
    row_copy = pltpu.make_async_copy(row_ref, place_ref, sems.at[QUARTERS])
    row_copy.start()
    first_copy.wait()
    for group in range(QUARTERS):
        lanes = slice(group * LANES, (group + 1) * LANES)
        turned_ref[lanes, 0:TB] = first_ref[:, lanes].T
    parts = [turned_ref[pl.ds(k, DEVICES, stride=4), :] for k in range(4)]
    send_ref[pl.ds(SLOTS * 8, DEVICES, stride=MSG), :] = exchange_chunks(parts)[0]
    copies[0].wait()
    row_copy.wait()
    for group in range(QUARTERS):
        if group:
            copies[group].wait()
        parts = [amp_ref[group, pl.ds(k, DEVICES, stride=4), :] for k in range(4)]
        for h, tiles in enumerate(exchange_chunks(parts)):
            for upper in range(NVT):
                row = place_ref[0, upper * NVT + group * 4 + h]
                send_ref[pl.ds(row, 8), :] = tiles[upper * 8 : (upper + 1) * 8]
    head_copy.wait()


def pack(table, amplitudes, integrals):
    hbm = pl.BlockSpec(memory_space=pltpu.HBM)
    return pl.pallas_call(
        pack_kernel,
        out_shape=(
            jax.ShapeDtypeStruct((DEVICES * MSG, LANES), F32),
            jax.ShapeDtypeStruct((PAIR, PAIR), F32),
        ),
        in_specs=[hbm, hbm, hbm],
        out_specs=(pl.BlockSpec(memory_space=pltpu.VMEM),) * 2,
        scratch_shapes=[
            pltpu.VMEM((SLOTS, 2, DEVICES), jnp.int32),
            pltpu.VMEM((1, TILES), jnp.int32),
            pltpu.SMEM((1, TILES), jnp.int32),
            pltpu.VMEM((TB, V), F32),
            pltpu.VMEM((QUARTERS, V, LANES), F32),
            pltpu.VMEM((V, LANES), F32),
            pltpu.SemaphoreType.DMA((QUARTERS + 3,)),
        ],
        compiler_params=pltpu.CompilerParams(vmem_limit_bytes=16 * 1024 * 1024),
        name="pack",
    )(
        pltpu.with_memory_space_constraint(table, pltpu.HBM),
        pltpu.with_memory_space_constraint(amplitudes, pltpu.HBM),
        pltpu.with_memory_space_constraint(integrals, pltpu.HBM),
    )


def nt_dot(a, b):
    return lax.dot_general(a, b, (((1,), (1,)), ((), ())), preferred_element_type=F32)


def nn_dot(a, b):
    return lax.dot_general(a, b, (((1,), (0,)), ((), ())), preferred_element_type=F32)


def split_parts(value):
    high = value.astype(BF16)
    return high, (value - high.astype(F32)).astype(BF16)


PIECE = 256
HALF = DEVICES // 2


def main_kernel(
    table_hbm,
    recv_ref,
    head_ref,
    int_hbm,
    coup_ref,
    own_ref,
    other_ref,
    table_ref,
    int_ref,
    both_ref,
    acc_ref,
    hole_ref,
    turned_ref,
    sems,
):
    table_copy = pltpu.make_async_copy(table_hbm, table_ref, sems.at[SLOTS])
    table_copy.start()

    def fetch(slot):
        return pltpu.make_async_copy(int_hbm.at[slot], int_ref.at[slot - 1], sems.at[slot])

    fetch(1).start()
    core = lax.axis_index("col_1")

    def prepare(slot):
        for m in range(8):
            lanes = slice(m * LANES, (m + 1) * LANES)
            for half, parity in enumerate((core, 1 - core)):
                part = recv_ref[pl.ds(parity * MSG + slot * 8 + m, HALF, stride=2 * MSG), :]
                high, low = split_parts(part)
                both_ref[slot, half * HALF : (half + 1) * HALF, lanes] = high
                both_ref[slot, DEVICES + half * HALF : DEVICES + (half + 1) * HALF, lanes] = low

    def product(slot, values):
        int_high, int_low = split_parts(values)
        top = nt_dot(int_high, both_ref[slot])
        low = nt_dot(int_low, both_ref[slot, 0:DEVICES, :])
        return top[:, :DEVICES] + top[:, DEVICES:] + low

    pieces = [slice(first, first + PIECE) for first in range(0, PAIR, PIECE)]
    prepare(0)
    table_copy.wait()
    own = lax.axis_index(ROW_COL)
    count = jnp.int32(0)
    for s in range(SLOTS):
        count += (table_ref[s, 0, own] >= 0).astype(jnp.int32)
    @pl.when(count > 2)
    def _():
        fetch(2).start()

    data = recv_ref[pl.ds(SLOTS * 8, DEVICES, stride=MSG), :]
    blocks = exchange_chunks([data[i * TB : (i + 1) * TB] for i in range(4)])
    left_high, left_low = split_parts(jnp.concatenate(blocks, axis=0).T)
    right_high, right_low = split_parts(coup_ref[...])
    hole = nn_dot(left_high, right_high) + nn_dot(left_low, right_high) + nn_dot(left_high, right_low)
    for group in range(8):
        hole_ref[group] = hole[:, group * LANES : (group + 1) * LANES]
    for group in range(8):
        parts = [hole_ref[group, pl.ds(k, DEVICES // 4, stride=4), :] for k in range(4)]
        for h, tiles in enumerate(exchange_chunks(parts)):
            for i in range(4):
                row = (i * TB + group * 4 + h) // 2 * 8
                half = h % 2 + core - 2 * (h % 2) * core
                turned_ref[pl.ds(half * (HALF * 8) + row, 8), :] = tiles[i * 8 : (i + 1) * 8]

    for rows in pieces:
        acc_ref[rows, :] = jnp.where(count > 0, product(0, head_ref[rows, :]), 0.0)
    @pl.when(count > 3)
    def _():
        fetch(3).start()

    fetch(1).wait()

    def add_slot(slot, _):
        prepare(slot)

        @pl.when(slot > 1)
        def _():
            fetch(slot).wait()

        for rows in pieces:
            acc_ref[rows, :] += product(slot, int_ref[slot - 1, rows, :])
        return 0

    lax.fori_loop(1, count, add_slot, 0)
    for m in range(8):
        ladder = acc_ref[m * LANES : (m + 1) * LANES, :].T
        for half, out_ref in enumerate((own_ref, other_ref)):
            hole = turned_ref[pl.ds(half * (HALF * 8) + m, HALF, stride=8), :]
            out_ref[pl.ds(m, HALF, stride=8), :] = hole + ladder[half * HALF : (half + 1) * HALF]


def partial_residual(table, received, head, integrals, coupling):
    whole = pl.BlockSpec(memory_space=pltpu.VMEM)
    hbm = pl.BlockSpec(memory_space=pltpu.HBM)
    return pl.pallas_call(
        main_kernel,
        out_shape=(jax.ShapeDtypeStruct((HALF * 8, LANES), F32),) * 2,
        in_specs=[hbm, whole, whole, hbm, whole],
        out_specs=(whole, whole),
        scratch_shapes=[
            pltpu.SMEM((SLOTS, 2, DEVICES), jnp.int32),
            pltpu.VMEM((SLOTS - 1, PAIR, PAIR), F32),
            pltpu.VMEM((SLOTS, 2 * DEVICES, PAIR), BF16),
            pltpu.VMEM((PAIR, DEVICES), F32),
            pltpu.VMEM((8, DEVICES, LANES), F32),
            pltpu.VMEM((DEVICES * 8, LANES), F32),
            pltpu.SemaphoreType.DMA((SLOTS + 1,)),
        ],
        compiler_params=pltpu.CompilerParams(vmem_limit_bytes=40 * 1024 * 1024),
        name="residual",
    )(
        pltpu.with_memory_space_constraint(table, pltpu.HBM),
        received,
        head,
        pltpu.with_memory_space_constraint(integrals, pltpu.HBM),
        coupling,
    )


def body(amplitudes, integrals, coupling, task_table):
    table = jnp.transpose(task_table, (1, 2, 0))
    outgoing, head = pack(table, amplitudes.reshape(V, V), integrals)
    received = lax.all_to_all(
        outgoing.reshape(DEVICES, MSG, 1, LANES), ROW_COL, split_axis=0, concat_axis=0, tiled=True
    ).reshape(DEVICES * MSG, LANES)
    own, other = partial_residual(table, received, head, integrals, coupling.reshape(LANES, PAIR))
    arrived = lax.ppermute(other, "col_1", [(0, 1), (1, 0)])
    chip = (own + arrived).reshape(HALF, 8, LANES)
    terms = lax.all_to_all(chip, ROW_COL[:3], split_axis=0, concat_axis=0, tiled=True)
    return jnp.sum(terms, axis=0).reshape(1, PAIR)


def solution(mesh):
    split = Mesh(mesh.devices.reshape(4, 4, 4, 2), ("row_0", "row_1", "col_0", "col_1"))
    in_specs = (P(ROW_COL, None, None), P(ROW_COL, None, None), P(ROW_COL, None, None), P())
    return jax.shard_map(body, mesh=split, in_specs=in_specs, out_specs=P(ROW_COL, None), check_vma=False)
```

```python
import functools

import jax
import jax.numpy as jnp
from jax import lax
from jax.experimental import pallas as pl
from jax.experimental.pallas import tpu as pltpu
from jax.sharding import Mesh
from jax.sharding import PartitionSpec as P

TB = 32
NVT = 16
SLOTS = 4
DEVICES = 128
V = 512
PAIR = TB * TB
LANES = 128
MSG = SLOTS * 8 + 1
ROW_COL = ("row_0", "row_1", "col_0", "col_1")
F32 = jnp.float32
BF16 = jnp.bfloat16


def exchange_chunks(parts):
    lane = lax.broadcasted_iota(jnp.int32, parts[0].shape, parts[0].ndim - 1)
    odd = (lane // TB) % 2 == 1
    high = lane >= 2 * TB
    axis = parts[0].ndim - 1

    def swap(a, b, mask, shift):
        return (
            jnp.where(mask, pltpu.roll(b, shift, axis), a),
            jnp.where(mask, b, pltpu.roll(a, LANES - shift, axis)),
        )

    c0, c1 = swap(parts[0], parts[1], odd, TB)
    c2, c3 = swap(parts[2], parts[3], odd, TB)
    b0, b2 = swap(c0, c2, high, 2 * TB)
    b1, b3 = swap(c1, c3, high, 2 * TB)
    return b0, b1, b2, b3


QUARTERS = V // LANES
TILES = NVT * NVT


def pack_kernel(
    table_hbm, amp_hbm, int_hbm, send_ref, head_ref, table_ref, row_ref, place_ref, first_ref, amp_ref, turned_ref, sems
):
    head_copy = pltpu.make_async_copy(int_hbm.at[0], head_ref, sems.at[QUARTERS + 1])
    table_copy = pltpu.make_async_copy(table_hbm, table_ref, sems.at[QUARTERS])
    table_copy.start()
    first_copy = pltpu.make_async_copy(amp_hbm.at[pl.ds(0, TB), :], first_ref, sems.at[QUARTERS + 2])
    first_copy.start()
    copies = []
    for group in range(QUARTERS):
        lanes = pl.ds(group * LANES, LANES)
        copies.append(pltpu.make_async_copy(amp_hbm.at[:, lanes], amp_ref.at[group], sems.at[group]))
        copies[-1].start()
    head_copy.start()
    table_copy.wait()
    sublane = lax.broadcasted_iota(jnp.int32, (8, DEVICES), 0)
    device = lax.broadcasted_iota(jnp.int32, (8, DEVICES), 1)
    tiles = lax.broadcasted_iota(jnp.int32, (TILES, DEVICES), 0)
    found = jnp.zeros((8, TILES), F32)
    for s in range(SLOTS):
        pair = table_ref[s, 0:1, :] * NVT + table_ref[s, 1:2, :]
        match = (tiles == pair).astype(F32).astype(BF16)
        found += nt_dot(jnp.where(sublane == 0, device, s).astype(F32).astype(BF16), match)
    row_ref[...] = (found[0:1] * MSG + found[1:2] * 8).astype(jnp.int32)
    row_copy = pltpu.make_async_copy(row_ref, place_ref, sems.at[QUARTERS])
    row_copy.start()
    first_copy.wait()
    for group in range(QUARTERS):
        lanes = slice(group * LANES, (group + 1) * LANES)
        turned_ref[lanes, 0:TB] = first_ref[:, lanes].T
    parts = [turned_ref[pl.ds(k, DEVICES, stride=4), :] for k in range(4)]
    send_ref[pl.ds(SLOTS * 8, DEVICES, stride=MSG), :] = exchange_chunks(parts)[0]
    copies[0].wait()
    row_copy.wait()
    for group in range(QUARTERS):
        if group:
            copies[group].wait()
        parts = [amp_ref[group, pl.ds(k, DEVICES, stride=4), :] for k in range(4)]
        for h, tiles in enumerate(exchange_chunks(parts)):
            for upper in range(NVT):
                row = place_ref[0, upper * NVT + group * 4 + h]
                send_ref[pl.ds(row, 8), :] = tiles[upper * 8 : (upper + 1) * 8]
    head_copy.wait()


def pack(table, amplitudes, integrals):
    hbm = pl.BlockSpec(memory_space=pltpu.HBM)
    return pl.pallas_call(
        pack_kernel,
        out_shape=(
            jax.ShapeDtypeStruct((DEVICES * MSG, LANES), F32),
            jax.ShapeDtypeStruct((PAIR, PAIR), F32),
        ),
        in_specs=[hbm, hbm, hbm],
        out_specs=(pl.BlockSpec(memory_space=pltpu.VMEM),) * 2,
        scratch_shapes=[
            pltpu.VMEM((SLOTS, 2, DEVICES), jnp.int32),
            pltpu.VMEM((1, TILES), jnp.int32),
            pltpu.SMEM((1, TILES), jnp.int32),
            pltpu.VMEM((TB, V), F32),
            pltpu.VMEM((QUARTERS, V, LANES), F32),
            pltpu.VMEM((V, LANES), F32),
            pltpu.SemaphoreType.DMA((QUARTERS + 3,)),
        ],
        compiler_params=pltpu.CompilerParams(vmem_limit_bytes=16 * 1024 * 1024),
        name="pack",
    )(
        pltpu.with_memory_space_constraint(table, pltpu.HBM),
        pltpu.with_memory_space_constraint(amplitudes, pltpu.HBM),
        pltpu.with_memory_space_constraint(integrals, pltpu.HBM),
    )


def nt_dot(a, b):
    return lax.dot_general(a, b, (((1,), (1,)), ((), ())), preferred_element_type=F32)


def nn_dot(a, b):
    return lax.dot_general(a, b, (((1,), (0,)), ((), ())), preferred_element_type=F32)


def split_parts(value):
    high = value.astype(BF16)
    return high, (value - high.astype(F32)).astype(BF16)


PIECE = 256
HALF = DEVICES // 2


def main_kernel(
    table_hbm,
    recv_ref,
    head_ref,
    int_hbm,
    coup_ref,
    own_ref,
    other_ref,
    table_ref,
    int_ref,
    both_ref,
    acc_ref,
    hole_ref,
    turned_ref,
    sems,
):
    table_copy = pltpu.make_async_copy(table_hbm, table_ref, sems.at[SLOTS])
    table_copy.start()

    def fetch(slot):
        return pltpu.make_async_copy(int_hbm.at[slot], int_ref.at[slot - 1], sems.at[slot])

    fetch(1).start()
    core = lax.axis_index("col_1")

    def prepare(slot):
        for m in range(8):
            lanes = slice(m * LANES, (m + 1) * LANES)
            for half, parity in enumerate((core, 1 - core)):
                part = recv_ref[pl.ds(parity * MSG + slot * 8 + m, HALF, stride=2 * MSG), :]
                high, low = split_parts(part)
                both_ref[slot, half * HALF : (half + 1) * HALF, lanes] = high
                both_ref[slot, DEVICES + half * HALF : DEVICES + (half + 1) * HALF, lanes] = low

    def product(slot, values):
        int_high, int_low = split_parts(values)
        top = nt_dot(int_high, both_ref[slot])
        low = nt_dot(int_low, both_ref[slot, 0:DEVICES, :])
        return top[:, :DEVICES] + top[:, DEVICES:] + low

    pieces = [slice(first, first + PIECE) for first in range(0, PAIR, PIECE)]
    for slot in range(SLOTS):
        prepare(slot)
    table_copy.wait()
    own = lax.axis_index(ROW_COL)
    count = jnp.int32(0)
    for s in range(SLOTS):
        count += (table_ref[s, 0, own] >= 0).astype(jnp.int32)
    for slot in range(2, SLOTS):

        @pl.when(slot < count)
        def _():
            fetch(slot).start()

    data = recv_ref[pl.ds(SLOTS * 8, DEVICES, stride=MSG), :]
    blocks = exchange_chunks([data[i * TB : (i + 1) * TB] for i in range(4)])
    left_high, left_low = split_parts(jnp.concatenate(blocks, axis=0).T)
    right_high, right_low = split_parts(coup_ref[...])
    hole = nn_dot(left_high, right_high) + nn_dot(left_low, right_high) + nn_dot(left_high, right_low)
    for group in range(8):
        hole_ref[group] = hole[:, group * LANES : (group + 1) * LANES]
    for group in range(8):
        parts = [hole_ref[group, pl.ds(k, DEVICES // 4, stride=4), :] for k in range(4)]
        for h, tiles in enumerate(exchange_chunks(parts)):
            for i in range(4):
                row = (i * TB + group * 4 + h) // 2 * 8
                half = h % 2 + core - 2 * (h % 2) * core
                turned_ref[pl.ds(half * (HALF * 8) + row, 8), :] = tiles[i * 8 : (i + 1) * 8]

    for rows in pieces:
        acc_ref[rows, :] = jnp.where(count > 0, product(0, head_ref[rows, :]), 0.0)
    fetch(1).wait()

    def add_slot(slot, _):
        @pl.when(slot > 1)
        def _():
            fetch(slot).wait()

        for rows in pieces:
            acc_ref[rows, :] += product(slot, int_ref[slot - 1, rows, :])
        return 0

    lax.fori_loop(1, count, add_slot, 0)
    for m in range(8):
        ladder = acc_ref[m * LANES : (m + 1) * LANES, :].T
        for half, out_ref in enumerate((own_ref, other_ref)):
            hole = turned_ref[pl.ds(half * (HALF * 8) + m, HALF, stride=8), :]
            out_ref[pl.ds(m, HALF, stride=8), :] = hole + ladder[half * HALF : (half + 1) * HALF]


def partial_residual(table, received, head, integrals, coupling):
    whole = pl.BlockSpec(memory_space=pltpu.VMEM)
    hbm = pl.BlockSpec(memory_space=pltpu.HBM)
    return pl.pallas_call(
        main_kernel,
        out_shape=(jax.ShapeDtypeStruct((HALF * 8, LANES), F32),) * 2,
        in_specs=[hbm, whole, whole, hbm, whole],
        out_specs=(whole, whole),
        scratch_shapes=[
            pltpu.SMEM((SLOTS, 2, DEVICES), jnp.int32),
            pltpu.VMEM((SLOTS - 1, PAIR, PAIR), F32),
            pltpu.VMEM((SLOTS, 2 * DEVICES, PAIR), BF16),
            pltpu.VMEM((PAIR, DEVICES), F32),
            pltpu.VMEM((8, DEVICES, LANES), F32),
            pltpu.VMEM((DEVICES * 8, LANES), F32),
            pltpu.SemaphoreType.DMA((SLOTS + 1,)),
        ],
        compiler_params=pltpu.CompilerParams(vmem_limit_bytes=40 * 1024 * 1024),
        name="residual",
    )(
        pltpu.with_memory_space_constraint(table, pltpu.HBM),
        received,
        head,
        pltpu.with_memory_space_constraint(integrals, pltpu.HBM),
        coupling,
    )


def body(amplitudes, integrals, coupling, task_table):
    table = jnp.transpose(task_table, (1, 2, 0))
    outgoing, head = pack(table, amplitudes.reshape(V, V), integrals)
    received = lax.all_to_all(
        outgoing.reshape(DEVICES, MSG, 1, LANES), ROW_COL, split_axis=0, concat_axis=0, tiled=True
    ).reshape(DEVICES * MSG, LANES)
    own, other = partial_residual(table, received, head, integrals, coupling.reshape(LANES, PAIR))
    arrived = lax.ppermute(other, "col_1", [(0, 1), (1, 0)])
    chip = (own + arrived).reshape(HALF, 8, LANES)
    terms = lax.all_to_all(chip, ROW_COL[:3], split_axis=0, concat_axis=0, tiled=True)
    return jnp.sum(terms, axis=0).reshape(1, PAIR)


def solution(mesh):
    split = Mesh(mesh.devices.reshape(4, 4, 4, 2), ("row_0", "row_1", "col_0", "col_1"))
    in_specs = (P(ROW_COL, None, None), P(ROW_COL, None, None), P(ROW_COL, None, None), P())
    return jax.shard_map(body, mesh=split, in_specs=in_specs, out_specs=P(ROW_COL, None), check_vma=False)
```

```python
import functools

import jax
import jax.numpy as jnp
from jax import lax
from jax.experimental import pallas as pl
from jax.experimental.pallas import tpu as pltpu
from jax.sharding import Mesh
from jax.sharding import PartitionSpec as P

TB = 32
NVT = 16
SLOTS = 4
DEVICES = 128
V = 512
PAIR = TB * TB
LANES = 128
MSG = SLOTS * 8 + 1
ROW_COL = ("row_0", "row_1", "col_0", "col_1")
F32 = jnp.float32
BF16 = jnp.bfloat16


def exchange_chunks(parts):
    lane = lax.broadcasted_iota(jnp.int32, parts[0].shape, parts[0].ndim - 1)
    odd = (lane // TB) % 2 == 1
    high = lane >= 2 * TB
    axis = parts[0].ndim - 1

    def swap(a, b, mask, shift):
        return (
            jnp.where(mask, pltpu.roll(b, shift, axis), a),
            jnp.where(mask, b, pltpu.roll(a, LANES - shift, axis)),
        )

    c0, c1 = swap(parts[0], parts[1], odd, TB)
    c2, c3 = swap(parts[2], parts[3], odd, TB)
    b0, b2 = swap(c0, c2, high, 2 * TB)
    b1, b3 = swap(c1, c3, high, 2 * TB)
    return b0, b1, b2, b3


QUARTERS = V // LANES
TILES = NVT * NVT


def pack_kernel(
    table_hbm, amp_hbm, int_hbm, send_ref, head_ref, table_ref, row_ref, place_ref, first_ref, amp_ref, turned_ref, sems
):
    head_copy = pltpu.make_async_copy(int_hbm.at[0], head_ref, sems.at[QUARTERS + 1])
    table_copy = pltpu.make_async_copy(table_hbm, table_ref, sems.at[QUARTERS])
    table_copy.start()
    first_copy = pltpu.make_async_copy(amp_hbm.at[pl.ds(0, TB), :], first_ref, sems.at[QUARTERS + 2])
    first_copy.start()
    copies = []
    for group in range(QUARTERS):
        lanes = pl.ds(group * LANES, LANES)
        copies.append(pltpu.make_async_copy(amp_hbm.at[:, lanes], amp_ref.at[group], sems.at[group]))
        copies[-1].start()
    head_copy.start()
    table_copy.wait()
    sublane = lax.broadcasted_iota(jnp.int32, (8, DEVICES), 0)
    device = lax.broadcasted_iota(jnp.int32, (8, DEVICES), 1)
    tiles = lax.broadcasted_iota(jnp.int32, (TILES, DEVICES), 0)
    found = jnp.zeros((8, TILES), F32)
    for s in range(SLOTS):
        pair = table_ref[s, 0:1, :] * NVT + table_ref[s, 1:2, :]
        match = (tiles == pair).astype(F32).astype(BF16)
        found += nt_dot(jnp.where(sublane == 0, device, s).astype(F32).astype(BF16), match)
    row_ref[...] = (found[0:1] * MSG + found[1:2] * 8).astype(jnp.int32)
    row_copy = pltpu.make_async_copy(row_ref, place_ref, sems.at[QUARTERS])
    row_copy.start()
    first_copy.wait()
    for group in range(QUARTERS):
        lanes = slice(group * LANES, (group + 1) * LANES)
        turned_ref[lanes, 0:TB] = first_ref[:, lanes].T
    parts = [turned_ref[pl.ds(k, DEVICES, stride=4), :] for k in range(4)]
    send_ref[pl.ds(SLOTS * 8, DEVICES, stride=MSG), :] = exchange_chunks(parts)[0]
    copies[0].wait()
    row_copy.wait()
    for group in range(QUARTERS):
        if group:
            copies[group].wait()
        parts = [amp_ref[group, pl.ds(k, DEVICES, stride=4), :] for k in range(4)]
        for h, tiles in enumerate(exchange_chunks(parts)):
            for upper in range(NVT):
                row = place_ref[0, upper * NVT + group * 4 + h]
                send_ref[pl.ds(row, 8), :] = tiles[upper * 8 : (upper + 1) * 8]
    head_copy.wait()


def pack(table, amplitudes, integrals):
    hbm = pl.BlockSpec(memory_space=pltpu.HBM)
    return pl.pallas_call(
        pack_kernel,
        out_shape=(
            jax.ShapeDtypeStruct((DEVICES * MSG, LANES), F32),
            jax.ShapeDtypeStruct((PAIR, PAIR), F32),
        ),
        in_specs=[hbm, hbm, hbm],
        out_specs=(pl.BlockSpec(memory_space=pltpu.VMEM),) * 2,
        scratch_shapes=[
            pltpu.VMEM((SLOTS, 2, DEVICES), jnp.int32),
            pltpu.VMEM((1, TILES), jnp.int32),
            pltpu.SMEM((1, TILES), jnp.int32),
            pltpu.VMEM((TB, V), F32),
            pltpu.VMEM((QUARTERS, V, LANES), F32),
            pltpu.VMEM((V, LANES), F32),
            pltpu.SemaphoreType.DMA((QUARTERS + 3,)),
        ],
        compiler_params=pltpu.CompilerParams(vmem_limit_bytes=16 * 1024 * 1024),
        name="pack",
    )(
        pltpu.with_memory_space_constraint(table, pltpu.HBM),
        pltpu.with_memory_space_constraint(amplitudes, pltpu.HBM),
        pltpu.with_memory_space_constraint(integrals, pltpu.HBM),
    )


def nt_dot(a, b):
    return lax.dot_general(a, b, (((1,), (1,)), ((), ())), preferred_element_type=F32)


def nn_dot(a, b):
    return lax.dot_general(a, b, (((1,), (0,)), ((), ())), preferred_element_type=F32)


def split_parts(value):
    high = value.astype(BF16)
    return high, (value - high.astype(F32)).astype(BF16)


PIECE = 256
HALF = DEVICES // 2


def main_kernel(
    table_hbm,
    recv_ref,
    head_ref,
    int_hbm,
    coup_ref,
    own_ref,
    other_ref,
    table_ref,
    int_ref,
    both_ref,
    acc_ref,
    hole_ref,
    turned_ref,
    sems,
):
    table_copy = pltpu.make_async_copy(table_hbm, table_ref, sems.at[SLOTS])
    table_copy.start()

    def fetch(slot):
        return pltpu.make_async_copy(int_hbm.at[slot], int_ref.at[slot - 1], sems.at[slot])

    fetch(1).start()
    core = lax.axis_index("col_1")

    def prepare(slot):
        for m in range(8):
            lanes = slice(m * LANES, (m + 1) * LANES)
            for half, parity in enumerate((core, 1 - core)):
                part = recv_ref[pl.ds(parity * MSG + slot * 8 + m, HALF, stride=2 * MSG), :]
                high, low = split_parts(part)
                both_ref[slot, half * HALF : (half + 1) * HALF, lanes] = high
                both_ref[slot, DEVICES + half * HALF : DEVICES + (half + 1) * HALF, lanes] = low

    def product(slot, values):
        int_high, int_low = split_parts(values)
        top = nt_dot(int_high, both_ref[slot])
        low = nt_dot(int_low, both_ref[slot, 0:DEVICES, :])
        return top[:, :DEVICES] + top[:, DEVICES:] + low

    pieces = [slice(first, first + PIECE) for first in range(0, PAIR, PIECE)]
    for slot in range(SLOTS):
        prepare(slot)
    table_copy.wait()
    own = lax.axis_index(ROW_COL)
    count = jnp.int32(0)
    for s in range(SLOTS):
        count += (table_ref[s, 0, own] >= 0).astype(jnp.int32)
    for slot in range(2, SLOTS):

        @pl.when(slot < count)
        def _():
            fetch(slot).start()

    data = recv_ref[pl.ds(SLOTS * 8, DEVICES, stride=MSG), :]
    blocks = exchange_chunks([data[i * TB : (i + 1) * TB] for i in range(4)])
    left_high, left_low = split_parts(jnp.concatenate(blocks, axis=0).T)
    right_high, right_low = split_parts(coup_ref[...])
    hole = nn_dot(left_high, right_high) + nn_dot(left_low, right_high) + nn_dot(left_high, right_low)
    for group in range(8):
        hole_ref[group] = hole[:, group * LANES : (group + 1) * LANES]
    for group in range(8):
        parts = [hole_ref[group, pl.ds(k, DEVICES // 4, stride=4), :] for k in range(4)]
        for h, tiles in enumerate(exchange_chunks(parts)):
            for i in range(4):
                row = (i * TB + group * 4 + h) // 2 * 8
                half = h % 2 + core - 2 * (h % 2) * core
                turned_ref[pl.ds(half * (HALF * 8) + row, 8), :] = tiles[i * 8 : (i + 1) * 8]

    for rows in pieces:
        acc_ref[rows, :] = jnp.where(count > 0, product(0, head_ref[rows, :]), 0.0)
    fetch(1).wait()

    for slot in range(1, SLOTS):

        @pl.when(slot < count)
        def _():
            if slot > 1:
                fetch(slot).wait()
            for rows in pieces:
                acc_ref[rows, :] += product(slot, int_ref[slot - 1, rows, :])

    for m in range(8):
        ladder = acc_ref[m * LANES : (m + 1) * LANES, :].T
        for half, out_ref in enumerate((own_ref, other_ref)):
            hole = turned_ref[pl.ds(half * (HALF * 8) + m, HALF, stride=8), :]
            out_ref[pl.ds(m, HALF, stride=8), :] = hole + ladder[half * HALF : (half + 1) * HALF]


def partial_residual(table, received, head, integrals, coupling):
    whole = pl.BlockSpec(memory_space=pltpu.VMEM)
    hbm = pl.BlockSpec(memory_space=pltpu.HBM)
    return pl.pallas_call(
        main_kernel,
        out_shape=(jax.ShapeDtypeStruct((HALF * 8, LANES), F32),) * 2,
        in_specs=[hbm, whole, whole, hbm, whole],
        out_specs=(whole, whole),
        scratch_shapes=[
            pltpu.SMEM((SLOTS, 2, DEVICES), jnp.int32),
            pltpu.VMEM((SLOTS - 1, PAIR, PAIR), F32),
            pltpu.VMEM((SLOTS, 2 * DEVICES, PAIR), BF16),
            pltpu.VMEM((PAIR, DEVICES), F32),
            pltpu.VMEM((8, DEVICES, LANES), F32),
            pltpu.VMEM((DEVICES * 8, LANES), F32),
            pltpu.SemaphoreType.DMA((SLOTS + 1,)),
        ],
        compiler_params=pltpu.CompilerParams(vmem_limit_bytes=40 * 1024 * 1024),
        name="residual",
    )(
        pltpu.with_memory_space_constraint(table, pltpu.HBM),
        received,
        head,
        pltpu.with_memory_space_constraint(integrals, pltpu.HBM),
        coupling,
    )


def body(amplitudes, integrals, coupling, task_table):
    table = jnp.transpose(task_table, (1, 2, 0))
    outgoing, head = pack(table, amplitudes.reshape(V, V), integrals)
    received = lax.all_to_all(
        outgoing.reshape(DEVICES, MSG, 1, LANES), ROW_COL, split_axis=0, concat_axis=0, tiled=True
    ).reshape(DEVICES * MSG, LANES)
    own, other = partial_residual(table, received, head, integrals, coupling.reshape(LANES, PAIR))
    arrived = lax.ppermute(other, "col_1", [(0, 1), (1, 0)])
    chip = (own + arrived).reshape(HALF, 8, LANES)
    terms = lax.all_to_all(chip, ROW_COL[:3], split_axis=0, concat_axis=0, tiled=True)
    return jnp.sum(terms, axis=0).reshape(1, PAIR)


def solution(mesh):
    split = Mesh(mesh.devices.reshape(4, 4, 4, 2), ("row_0", "row_1", "col_0", "col_1"))
    in_specs = (P(ROW_COL, None, None), P(ROW_COL, None, None), P(ROW_COL, None, None), P())
    return jax.shard_map(body, mesh=split, in_specs=in_specs, out_specs=P(ROW_COL, None), check_vma=False)
```
